256 devices in a mesh: wide: 64 (over z, y, core), narrow: 4 (over x).
Axes of the slice: x: 4, y: 4, z: 8, core: 2. Of those that a mesh axis runs over, the one named last changes fastest.
Arguments:
- queries: bfloat16 [98304, 4096], P(('wide', 'narrow')), may hold values from -17 to 17
- output_gradient: bfloat16 [98304, 4096], P(('wide', 'narrow')), may hold values from -6 to 6
- response_keys: bfloat16 [98304, 512], P(('wide', 'narrow')), may hold values from -17 to 17
- response_values: bfloat16 [98304, 512], P(('wide', 'narrow')), may hold values from -6 to 6
- prompt_key_rows: bfloat16 [64, 256, 512], P('wide', 'narrow'), may hold values from -6 to 6
- prompt_value_rows: bfloat16 [64, 256, 512], P('wide', 'narrow'), may hold values from -6 to 6
- prompt_index: int32 [12288, 1], P(('wide', 'narrow')), may hold values from 0 to 63; in each aligned block of 48 rows (0 to 47, 48 to 95, ...) at most 2 rows name the same one
Outputs:
- query_grad: bfloat16 [98304, 4096], P(('wide', 'narrow'))
- response_key_gradient: bfloat16 [98304, 512], P(('wide', 'narrow'))
- response_value_gradient: bfloat16 [98304, 512], P(('wide', 'narrow'))
- prompt_key_grad: bfloat16 [64, 256, 512], P('wide', 'narrow')
- prompt_value_grad: bfloat16 [64, 256, 512], P('wide', 'narrow')
The draws below stay inside these ranges and needn't reach their ends.
Inputs may be any that keep to these rules, and one draw needn't show every extreme that they name: `prompt_index`: at most 2 of the responses held by one device have the same prompt.
All inputs are finite; a program needn't handle non-finite values.
Results may differ from the reference program's by a relative error of at most 0.015.
Values may be sent and summed in bfloat16 or wider, within the bound.
No kernel may reach another device: no remote copies, remote signals or barrier semaphores. Data moves between devices by JAX's collectives and lax.ppermute only.
A program may use at most 256 MiB of HBM per device.

```python
import math
import jax
import jax.numpy as jnp
import numpy as np
from jax import lax

QUERY_HEADS = 32
KEY_VALUE_HEADS = 4
HEAD_DIMENSION = 128
RESPONSE_LENGTH = 8
NR = 48
CAP = 2
PROMPT_LENGTH = 256
RESP = 12288
RESPONSE_TOKENS = 98304
N_WIDE = 64


def draw_queries(key, part):
    key = jax.random.fold_in(key, 1)
    return jnp.clip(jax.random.normal(key, (RESPONSE_TOKENS, QUERY_HEADS * HEAD_DIMENSION), jnp.float32), -4.0, 4.0).astype(jnp.bfloat16)


def draw_response_keys(key, part):
    key = jax.random.fold_in(key, 2)
    return jnp.clip(jax.random.normal(key, (RESPONSE_TOKENS, KEY_VALUE_HEADS * HEAD_DIMENSION), jnp.float32), -4.0, 4.0).astype(jnp.bfloat16)


def steps_of(own_key, extent, split, low, largest):
    factor_of = 1.0
    for position, parts in split:
        heights = jax.random.uniform(jax.random.fold_in(jax.random.fold_in(own_key, 6), position), (parts,), jnp.float32, low / len(split), largest / len(split))
        factor_of = factor_of * jnp.repeat(jnp.exp(heights), extent[position] // parts).reshape((-1,) + (1,) * (len(extent) - 1 - position))
    return factor_of


def shared_out(stream_key, own, number, rows, count, top, most, lean):
    sequence = jax.random.permutation(stream_key, count)
    packed, ordinary = portions_of(count, rows * top, most, lean, True), portions_of(count, rows * top, most, lean, False)
    places = jnp.arange(count)

    def named(lengths, offset_by):
        used = int((lengths > 0).sum())
        fixed = max(1, used // 4)
        shifted = fixed + (places - fixed + offset_by * (used - fixed)) % max(1, count - fixed)
        return jnp.zeros((count,), jnp.int32).at[sequence[jnp.where(places < fixed, places, shifted)]].set(jnp.asarray(lengths, jnp.int32))

    lengths = jnp.where(number % 4 == 0, named(packed, number // 4), named(ordinary, number - number // 4 - 1))
    mixed = jax.random.permutation(jax.random.fold_in(own, 3), count)
    giver, taker = mixed[0:count // 2 * 2:2], mixed[1:count // 2 * 2:2]
    slack = jnp.minimum(lengths[giver] - 1, most - lengths[taker]) // 2
    slack = jnp.where((giver == sequence[0]) | (taker == sequence[0]) | (lengths[taker] == 0), 0, jnp.maximum(slack, 0))
    shifted = jax.random.randint(jax.random.fold_in(own, 4), (count // 2,), 0, 1 << 20) % (slack + 1)
    lengths = lengths.at[giver].add(-shifted).at[taker].add(shifted)
    members = jnp.searchsorted(jnp.cumsum(lengths), jnp.arange(rows * top), side="right").astype(jnp.int32)
    grid = members.reshape(top, rows).T
    grid = grid[jax.random.permutation(jax.random.fold_in(own, 1), rows)]
    offset_by = jax.random.randint(jax.random.fold_in(own, 2), (rows, 1), 0, top)
    return jnp.take_along_axis(grid, (jnp.arange(top)[None, :] + offset_by) % top, axis=1)


def portions_of(amount, total, limit, skew, full):
    weights = [(1 << 20) // math.isqrt(rank ** skew) + 1 for rank in range(1, amount + 1)]
    largest = limit if full else min(limit, max(-(-total // amount), total * weights[0] // sum(weights)))
    least = 1 if total - largest >= amount - 1 else 0
    counts, surplus = [largest] + [least] * (amount - 1), total - largest - least * (amount - 1)
    while surplus > 0:
        movable = [i for i in range(1, amount) if counts[i] < largest] or [i for i in range(1, amount) if counts[i] < limit]
        pool, budget = sum([weights[i] for i in movable]), surplus
        for i in movable:
            more = min(limit - counts[i], max(1, budget * weights[i] // pool), surplus)
            counts[i] = counts[i] + more
            surplus = surplus - more
    return np.array(counts)


def bell_draw(rng, dims, spread, limit, shards=(), dtype=jnp.bfloat16):
    array = spread * jax.random.normal(rng, dims, jnp.float32)
    if shards:
        array = array * steps_of(rng, dims, shards, -0.22, 0.18)
    return jnp.clip(array, -limit, limit).astype(dtype)


def setup_inputs(seed: int = 0) -> dict:
    arg_keys = jax.random.split(jax.random.key(seed), 8)
    queries = draw_queries(jax.random.fold_in(arg_keys[7], 71), 0)
    output_gradient = bell_draw(arg_keys[1], (RESPONSE_TOKENS, QUERY_HEADS * HEAD_DIMENSION), 1.0, 6.0, ((0, 256),))
    response_keys = draw_response_keys(jax.random.fold_in(arg_keys[7], 71), 0)
    response_values = bell_draw(arg_keys[3], (RESPONSE_TOKENS, KEY_VALUE_HEADS * HEAD_DIMENSION), 1.0, 6.0, ((0, 256),))
    prompt_key_rows = bell_draw(arg_keys[4], (N_WIDE, PROMPT_LENGTH, KEY_VALUE_HEADS * HEAD_DIMENSION), 1.0, 6.0, ((0, 64), (1, 4)))
    prompt_value_rows = bell_draw(arg_keys[5], (N_WIDE, PROMPT_LENGTH, KEY_VALUE_HEADS * HEAD_DIMENSION), 1.0, 6.0, ((0, 64), (1, 4)))
    prompt_index_keys = jax.random.split(jax.random.fold_in(arg_keys[6], 1), RESP // NR)
    prompt_index_turns = jax.random.permutation(jax.random.fold_in(arg_keys[6], 3), RESP // NR)
    prompt_index = jax.vmap(lambda own, number: shared_out(jax.random.fold_in(arg_keys[6], 2), own, number, NR, N_WIDE, 1, CAP, 2))(prompt_index_keys, prompt_index_turns).reshape((RESP, 1))
    return dict(queries=queries, output_gradient=output_gradient, response_keys=response_keys, response_values=response_values, prompt_key_rows=prompt_key_rows, prompt_value_rows=prompt_value_rows, prompt_index=prompt_index)


def rounded(values):
    return lax.optimization_barrier(values.astype(jnp.bfloat16)).astype(jnp.float32)

def reference(queries, output_gradient, response_keys, response_values, prompt_key_rows, prompt_value_rows, prompt_index):
    queries_per_group = QUERY_HEADS // KEY_VALUE_HEADS
    scaling = 1.0 / math.sqrt(HEAD_DIMENSION)
    block_length = math.gcd(RESP, 64)
    block_count = RESP // block_length
    causal = jnp.arange(RESPONSE_LENGTH)[:, None] >= jnp.arange(RESPONSE_LENGTH)[None, :]

    def visit(loop_state, input_arrays):
        query_row_values, delta_row_values, key_row_values, value_row_values, owner_prompts = input_arrays
        full_queries = query_row_values.astype(jnp.float32).reshape(block_length, RESPONSE_LENGTH, KEY_VALUE_HEADS, queries_per_group, HEAD_DIMENSION)
        full_delta = delta_row_values.astype(jnp.float32).reshape(block_length, RESPONSE_LENGTH, KEY_VALUE_HEADS, queries_per_group, HEAD_DIMENSION)
        self_keys = key_row_values.astype(jnp.float32).reshape(block_length, RESPONSE_LENGTH, KEY_VALUE_HEADS, HEAD_DIMENSION)
        self_values = value_row_values.astype(jnp.float32).reshape(block_length, RESPONSE_LENGTH, KEY_VALUE_HEADS, HEAD_DIMENSION)
        prefix_keys = prompt_key_rows[owner_prompts].astype(jnp.float32).reshape(block_length, PROMPT_LENGTH, KEY_VALUE_HEADS, HEAD_DIMENSION)
        prefix_values = prompt_value_rows[owner_prompts].astype(jnp.float32).reshape(block_length, PROMPT_LENGTH, KEY_VALUE_HEADS, HEAD_DIMENSION)
        pre_scores = jnp.einsum('brhgd,bphd->brhgp', full_queries, prefix_keys) * scaling
        own_scores = jnp.einsum('brhgd,bshd->brhgs', full_queries, self_keys) * scaling
        own_scores = jnp.where(causal[None, :, None, None, :], own_scores, -jnp.inf)
        maxima = jnp.maximum(lax.optimization_barrier(jnp.max(pre_scores, axis=-1)), lax.optimization_barrier(jnp.max(own_scores, axis=-1)))
        totals = lax.optimization_barrier(jnp.sum(jnp.exp(pre_scores - maxima[..., None]), axis=-1)) + lax.optimization_barrier(jnp.sum(jnp.exp(own_scores - maxima[..., None]), axis=-1))
        log_norm = maxima + jnp.log(totals)
        pre_chance = jnp.exp(pre_scores - log_norm[..., None])
        own_chance = jnp.exp(own_scores - log_norm[..., None])
        pre_dots = jnp.einsum('brhgd,bphd->brhgp', full_delta, prefix_values)
        own_dots = jnp.einsum('brhgd,bshd->brhgs', full_delta, self_values)
        delta = lax.optimization_barrier(jnp.sum(pre_chance * pre_dots, axis=-1)) + lax.optimization_barrier(jnp.sum(own_chance * own_dots, axis=-1))
        pre_ds = rounded(pre_chance * (pre_dots - delta[..., None]))
        own_ds = rounded(own_chance * (own_dots - delta[..., None]))
        pre_weight = rounded(pre_chance)
        own_weight = rounded(own_chance)
        prompt_query = rounded(jnp.einsum('brhgp,bphd->brhgd', pre_ds, prefix_keys) * scaling)
        query_gradient = prompt_query + jnp.einsum('brhgs,bshd->brhgd', own_ds, self_keys) * scaling
        key_gradient = jnp.einsum('brhgs,brhgd->bshd', own_ds, full_queries) * scaling
        value_gradient = jnp.einsum('brhgs,brhgd->bshd', own_weight, full_delta)
        prompt_key_gradient = jnp.einsum('brhgp,brhgd->bphd', pre_ds, full_queries) * scaling
        prompt_value_gradient = jnp.einsum('brhgp,brhgd->bphd', pre_weight, full_delta)
        key_gradient_sum = loop_state[0].at[owner_prompts].add(prompt_key_gradient.reshape(block_length, PROMPT_LENGTH, KEY_VALUE_HEADS * HEAD_DIMENSION))
        value_gradient_sum = loop_state[1].at[owner_prompts].add(prompt_value_gradient.reshape(block_length, PROMPT_LENGTH, KEY_VALUE_HEADS * HEAD_DIMENSION))
        output_arrays = (query_gradient.reshape(block_length * RESPONSE_LENGTH, QUERY_HEADS * HEAD_DIMENSION).astype(jnp.bfloat16), key_gradient.reshape(block_length * RESPONSE_LENGTH, KEY_VALUE_HEADS * HEAD_DIMENSION).astype(jnp.bfloat16), value_gradient.reshape(block_length * RESPONSE_LENGTH, KEY_VALUE_HEADS * HEAD_DIMENSION).astype(jnp.bfloat16))
        return ((key_gradient_sum, value_gradient_sum), output_arrays)
    input_arrays = (queries.reshape(block_count, block_length * RESPONSE_LENGTH, QUERY_HEADS * HEAD_DIMENSION), output_gradient.reshape(block_count, block_length * RESPONSE_LENGTH, QUERY_HEADS * HEAD_DIMENSION), response_keys.reshape(block_count, block_length * RESPONSE_LENGTH, KEY_VALUE_HEADS * HEAD_DIMENSION), response_values.reshape(block_count, block_length * RESPONSE_LENGTH, KEY_VALUE_HEADS * HEAD_DIMENSION), prompt_index.reshape(block_count, block_length).astype(jnp.int32))
    start_offset = (jnp.zeros((N_WIDE, PROMPT_LENGTH, KEY_VALUE_HEADS * HEAD_DIMENSION), jnp.float32), jnp.zeros((N_WIDE, PROMPT_LENGTH, KEY_VALUE_HEADS * HEAD_DIMENSION), jnp.float32))
    sums, output_arrays = lax.scan(visit, start_offset, input_arrays)
    query_grad = output_arrays[0].reshape(RESPONSE_TOKENS, QUERY_HEADS * HEAD_DIMENSION)
    response_key_gradient = output_arrays[1].reshape(RESPONSE_TOKENS, KEY_VALUE_HEADS * HEAD_DIMENSION)
    response_value_gradient = output_arrays[2].reshape(RESPONSE_TOKENS, KEY_VALUE_HEADS * HEAD_DIMENSION)
    return (query_grad, response_key_gradient, response_value_gradient, sums[0].astype(jnp.bfloat16), sums[1].astype(jnp.bfloat16))
```

```python
import functools
import math

import jax
import jax.numpy as jnp
from jax import lax
from jax.experimental import pallas as pl
from jax.experimental.pallas import tpu as pltpu
from jax.sharding import PartitionSpec as P

QUERY_HEADS = 32
KEY_VALUE_HEADS = 4
PER_GROUP = QUERY_HEADS // KEY_VALUE_HEADS
HEAD = 128
TOKENS = 8
ROWS = PER_GROUP * TOKENS
SCALE = 1.0 / math.sqrt(HEAD)
LOG2E = math.log2(math.e)


def paired_order(targets):
    count = targets.shape[0]
    position = jnp.arange(count, dtype=jnp.int32)
    same = targets[:, None] == targets[None, :]
    before = position[None, :] < position[:, None]
    double = jnp.sum(same, axis=1) == 2
    first = jnp.logical_not(jnp.any(same & before, axis=1))
    head_of = jnp.sum(jnp.where(same & first[None, :], position[None, :], 0), axis=1)
    leads = double & first
    pair_rank = jnp.sum(leads[None, :] & (position[None, :] < head_of[:, None]), axis=1)
    single_rank = jnp.sum(jnp.logical_not(double)[None, :] & before, axis=1)
    slot = jnp.where(
        double,
        2 * pair_rank + jnp.logical_not(first).astype(jnp.int32),
        2 * jnp.sum(leads) + single_rank,
    )
    order = jnp.sum(jnp.where(slot[None, :] == position[:, None], position[None, :], 0), axis=1)
    owners = jnp.sum(jnp.where(slot[None, :] == position[:, None], targets[None, :], 0), axis=1)
    return order.astype(jnp.int32), owners.astype(jnp.int32)


def dot(left, right, contract):
    return lax.dot_general(left, right, (contract, ((), ())), preferred_element_type=jnp.float32)


def attend_kernel(
    order, owners, q_ref, d_ref, rk_ref, rv_ref, kv_ref,
    dq_ref, drk_ref, drv_ref, dkv_ref,
    q_rows, d_rows, own_k, own_v, dq_acc, drk_acc, drv_acc,
):
    responses = q_ref.shape[0] // TOKENS
    prompts = kv_ref.shape[0]

    def clear(g, _):
        dkv_ref[g] = jnp.zeros(dkv_ref.shape[1:], dkv_ref.dtype)
        return 0

    lax.fori_loop(0, prompts, clear, 0)
    own_k[...] = rk_ref[...].astype(jnp.float32)
    own_v[...] = rv_ref[...].astype(jnp.float32)

    def relay(p, _):
        lower = pl.multiple_of(p * 2 * TOKENS, 2 * TOKENS)
        for source, target in ((q_ref, q_rows), (d_ref, d_rows)):
            block = source[pl.ds(lower, 2 * TOKENS), :].astype(jnp.float32)
            stacked = jnp.concatenate(
                [
                    block[r * TOKENS : (r + 1) * TOKENS, h * HEAD : (h + 1) * HEAD]
                    for r in range(2)
                    for h in range(PER_GROUP)
                ],
                axis=0,
            )
            target[pl.ds(pl.multiple_of(p * 2 * ROWS, 2 * ROWS), 2 * ROWS), :] = stacked.astype(jnp.bfloat16)
        return 0

    lax.fori_loop(0, responses // 2, relay, 0)

    lanes = 2 * ROWS
    key_at = lax.broadcasted_iota(jnp.int32, (TOKENS, lanes), 0)
    token_at = lax.rem(lax.broadcasted_iota(jnp.int32, (TOKENS, lanes), 1), TOKENS)
    visible = key_at <= token_at
    none = jnp.zeros((ROWS, HEAD), jnp.bfloat16)
    blank = jnp.zeros((TOKENS, 2 * HEAD), jnp.float32)
    blank_lanes = jnp.zeros((TOKENS, lanes), jnp.float32)

    def both(a, b, axis):
        return jnp.concatenate([a, b], axis=axis)

    def visit(i, _):
        a, b = order[2 * i], order[2 * i + 1]
        ga, gb = owners[2 * i], owners[2 * i + 1]

        def spread(rows):
            first = rows[pl.ds(pl.multiple_of(a * ROWS, ROWS), ROWS), :]
            second = rows[pl.ds(pl.multiple_of(b * ROWS, ROWS), ROWS), :]
            return both(both(first, none, 1), both(none, second, 1), 0)

        at_a = pl.ds(pl.multiple_of(a * TOKENS, TOKENS), TOKENS)
        at_b = pl.ds(pl.multiple_of(b * TOKENS, TOKENS), TOKENS)
        q, d = spread(q_rows), spread(d_rows)
        k = both(kv_ref[ga, :, :HEAD], kv_ref[gb, :, :HEAD], 1)
        v = both(kv_ref[ga, :, HEAD:], kv_ref[gb, :, HEAD:], 1)
        ko = both(both(own_k[at_a, :], own_k[at_b, :], 1), blank, 0).astype(jnp.bfloat16)
        vo = both(both(own_v[at_a, :], own_v[at_b, :], 1), blank, 0).astype(jnp.bfloat16)
        across, along = ((1,), (1,)), ((1,), (0,))
        s = dot(k, q, across)
        t = dot(v, d, across)
        so = jnp.where(visible, dot(ko, q, across)[:TOKENS], -1e30)
        to = dot(vo, d, across)[:TOKENS]
        top = jnp.maximum(jnp.max(s, axis=0, keepdims=True), jnp.max(so, axis=0, keepdims=True))
        e = jnp.exp2((s - top) * (SCALE * LOG2E))
        eo = jnp.exp2((so - top) * (SCALE * LOG2E))
        total = jnp.sum(e, axis=0, keepdims=True) + jnp.sum(eo, axis=0, keepdims=True)
        mixed = jnp.sum(e * t, axis=0, keepdims=True) + jnp.sum(eo * to, axis=0, keepdims=True)
        inverse = 1.0 / total
        delta = mixed * inverse
        p = e * inverse
        po = eo * inverse
        w = p.astype(jnp.bfloat16)
        ds = (p * (t - delta)).astype(jnp.bfloat16)
        wo = both(po, blank_lanes, 0).astype(jnp.bfloat16)
        dso = both(po * (to - delta), blank_lanes, 0).astype(jnp.bfloat16)
        dk = dot(ds, q, along) * SCALE
        dv = dot(w, d, along)
        dko = dot(dso, q, along)[:TOKENS] * SCALE
        dvo = dot(wo, d, along)[:TOKENS]
        down = ((0,), (0,))
        dq = (dot(ds, k, down) + dot(dso, ko, down)) * SCALE
        for at, part in ((at_a, dq[:ROWS, :HEAD]), (at_b, dq[ROWS:, HEAD:])):
            dq_acc[at, :] = jnp.concatenate(
                [part[h * TOKENS : (h + 1) * TOKENS] for h in range(PER_GROUP)], axis=1
            )
        drk_acc[at_a, :] = dko[:, :HEAD]
        drk_acc[at_b, :] = dko[:, HEAD:]
        drv_acc[at_a, :] = dvo[:, :HEAD]
        drv_acc[at_b, :] = dvo[:, HEAD:]
        shared = (ga == gb).astype(jnp.float32)
        dkv_ref[gb] = both(dk[:, HEAD:], dv[:, HEAD:], 1).astype(jnp.bfloat16)
        dkv_ref[ga] = both(
            dk[:, :HEAD] + shared * dk[:, HEAD:], dv[:, :HEAD] + shared * dv[:, HEAD:], 1
        ).astype(jnp.bfloat16)
        return 0

    lax.fori_loop(0, responses // 2, visit, 0)
    dq_ref[...] = dq_acc[...].astype(jnp.bfloat16)
    drk_ref[...] = drk_acc[...].astype(jnp.bfloat16)
    drv_ref[...] = drv_acc[...].astype(jnp.bfloat16)


def attend(order, owners, queries, cotangents, keys, values, gathered, start, heads):
    rows = queries.shape[0]
    prompts, length, _ = gathered.shape
    wide = PER_GROUP * HEAD
    here = lambda shape: pl.BlockSpec(shape, lambda i, *_: (0, start + i))
    out = lambda shape: pl.BlockSpec(shape, lambda i, *_: (0, i))
    deep = pl.BlockSpec((prompts, length, 2 * HEAD), lambda i, *_: (0, 0, i))
    return pl.pallas_call(
        attend_kernel,
        grid_spec=pltpu.PrefetchScalarGridSpec(
            num_scalar_prefetch=2,
            grid=(heads,),
            in_specs=[here((rows, wide)), here((rows, wide)), here((rows, HEAD)), here((rows, HEAD)), deep],
            out_specs=[out((rows, wide)), out((rows, HEAD)), out((rows, HEAD)), deep],
            scratch_shapes=[
                pltpu.VMEM((rows * PER_GROUP, HEAD), jnp.bfloat16),
                pltpu.VMEM((rows * PER_GROUP, HEAD), jnp.bfloat16),
                pltpu.VMEM((rows, HEAD), jnp.float32),
                pltpu.VMEM((rows, HEAD), jnp.float32),
                pltpu.VMEM((rows, wide), jnp.float32),
                pltpu.VMEM((rows, HEAD), jnp.float32),
                pltpu.VMEM((rows, HEAD), jnp.float32),
            ],
        ),
        out_shape=[
            jax.ShapeDtypeStruct((rows, heads * wide), jnp.bfloat16),
            jax.ShapeDtypeStruct((rows, heads * HEAD), jnp.bfloat16),
            jax.ShapeDtypeStruct((rows, heads * HEAD), jnp.bfloat16),
            jax.ShapeDtypeStruct((prompts, length, heads * 2 * HEAD), jnp.bfloat16),
        ],
        compiler_params=pltpu.CompilerParams(vmem_limit_bytes=56 * 2**20),
        cost_estimate=pl.CostEstimate(
            flops=heads * 10 * rows * PER_GROUP * length * HEAD,
            bytes_accessed=heads * (4 * prompts * length * 2 * HEAD + 6 * rows * wide),
            transcendentals=heads * rows * PER_GROUP * length,
        ),
    )(order, owners, queries, cotangents, keys, values, gathered)


def by_head(keys, values):
    rows = keys.shape[0]
    keys = keys.reshape(rows, KEY_VALUE_HEADS, 1, HEAD)
    values = values.reshape(rows, KEY_VALUE_HEADS, 1, HEAD)
    return jnp.concatenate([keys, values], axis=2).reshape(rows, 2 * KEY_VALUE_HEADS * HEAD)


def body(queries, output_gradient, response_keys, response_values, prompt_key_rows, prompt_value_rows, prompt_index):
    prompts = lax.axis_size("wide")
    order, owners = paired_order(prompt_index[:, 0])
    held = by_head(prompt_key_rows[0], prompt_value_rows[0])
    gathered = lax.all_gather(held, ("wide", "narrow"), axis=0, tiled=True)
    gathered = gathered.reshape(prompts, -1, held.shape[1])
    dq, drk, drv, partial = attend(
        order, owners, queries, output_gradient, response_keys, response_values, gathered, 0, KEY_VALUE_HEADS
    )
    partial = partial.reshape(-1, held.shape[1])
    sums = lax.psum_scatter(partial, "wide", scatter_dimension=0, tiled=True)
    sums = lax.psum_scatter(sums, "narrow", scatter_dimension=0, tiled=True)
    split = sums.reshape(1, -1, KEY_VALUE_HEADS, 2, HEAD)
    shape = prompt_key_rows.shape
    return dq, drk, drv, split[:, :, :, 0].reshape(shape), split[:, :, :, 1].reshape(shape)


def solution(mesh):
    spread = P(("wide", "narrow"), None)
    prompt = P("wide", "narrow", None)
    return jax.shard_map(
        body,
        mesh=mesh,
        in_specs=(spread, spread, spread, spread, prompt, prompt, spread),
        out_specs=(spread, spread, spread, prompt, prompt),
        check_vma=False,
    )
```

```python
import functools
import math

import jax
import jax.numpy as jnp
from jax import lax
from jax.experimental import pallas as pl
from jax.experimental.pallas import tpu as pltpu
from jax.sharding import PartitionSpec as P

QUERY_HEADS = 32
KEY_VALUE_HEADS = 4
PER_GROUP = QUERY_HEADS // KEY_VALUE_HEADS
HEAD = 128
TOKENS = 8
ROWS = PER_GROUP * TOKENS
SCALE = 1.0 / math.sqrt(HEAD)
LOG2E = math.log2(math.e)


def paired_order(targets):
    count = targets.shape[0]
    position = jnp.arange(count, dtype=jnp.int32)
    same = targets[:, None] == targets[None, :]
    before = position[None, :] < position[:, None]
    double = jnp.sum(same, axis=1) == 2
    first = jnp.logical_not(jnp.any(same & before, axis=1))
    head_of = jnp.sum(jnp.where(same & first[None, :], position[None, :], 0), axis=1)
    leads = double & first
    pair_rank = jnp.sum(leads[None, :] & (position[None, :] < head_of[:, None]), axis=1)
    single_rank = jnp.sum(jnp.logical_not(double)[None, :] & before, axis=1)
    slot = jnp.where(
        double,
        2 * pair_rank + jnp.logical_not(first).astype(jnp.int32),
        2 * jnp.sum(leads) + single_rank,
    )
    order = jnp.sum(jnp.where(slot[None, :] == position[:, None], position[None, :], 0), axis=1)
    owners = jnp.sum(jnp.where(slot[None, :] == position[:, None], targets[None, :], 0), axis=1)
    return order.astype(jnp.int32), owners.astype(jnp.int32)


def dot(left, right, contract):
    return lax.dot_general(left, right, (contract, ((), ())), preferred_element_type=jnp.float32)

KEEP_SEND = (((0, 3), (1, 2)), ((0, 1), (3, 2)))
NEAR_FAR = ((1, 3), (3, 1))
BITS = {"x": 0, "c": 2, "y": 3, "z": 5}
FIRST = ("x", "y", "x", "y")


def attend_kernel(first, head, order, owners, spot, q_ref, d_ref, rk_ref, rv_ref, gathered, *refs):
    dq_ref, drk_ref, drv_ref = refs[:3]
    here_k, here_v, there, refs = refs[3:5], refs[5:7], refs[7:9], refs[9:]
    q_rows, d_rows, own_k, own_v, dq_acc, drk_acc, drv_acc, k_in, v_in, dk_out, dv_out, arrived, left = refs
    responses = q_ref.shape[0] // TOKENS

    def place(g):
        core, y, z = g & 1, (g >> 1) & 3, g >> 3
        return (core, slice(None), y, z) if first == "x" else (core, y, slice(None), z)

    fetches = [
        pltpu.make_async_copy(
            gathered.at[:, spot[0] ^ block, :, pl.ds((KEY_VALUE_HEADS * which + head) * HEAD, HEAD)],
            (k_in, v_in)[which].at[block],
            arrived,
        )
        for which in range(2)
        for block in range(4)
    ]
    for fetch in fetches:
        fetch.start()

    def clear(g, _):
        for target in (dk_out, dv_out):
            for core in range(2):
                for block in range(4):
                    target[core, block, :, g] = jnp.zeros((4,) + target.shape[4:], target.dtype)
        return 0

    lax.fori_loop(0, dk_out.shape[3], clear, 0)
    own_k[...] = rk_ref[...].astype(jnp.float32)
    own_v[...] = rv_ref[...].astype(jnp.float32)

    def relay(p, _):
        lower = pl.multiple_of(p * 2 * TOKENS, 2 * TOKENS)
        for source, target in ((q_ref, q_rows), (d_ref, d_rows)):
            block = source[pl.ds(lower, 2 * TOKENS), :].astype(jnp.float32)
            stacked = jnp.concatenate(
                [
                    block[r * TOKENS : (r + 1) * TOKENS, h * HEAD : (h + 1) * HEAD]
                    for r in range(2)
                    for h in range(PER_GROUP)
                ],
                axis=0,
            )
            target[pl.ds(pl.multiple_of(p * 2 * ROWS, 2 * ROWS), 2 * ROWS), :] = stacked.astype(jnp.bfloat16)
        return 0

    lax.fori_loop(0, responses // 2, relay, 0)
    for fetch in fetches:
        fetch.wait()

    lanes = 2 * ROWS
    key_at = lax.broadcasted_iota(jnp.int32, (TOKENS, lanes), 0)
    token_at = lax.rem(lax.broadcasted_iota(jnp.int32, (TOKENS, lanes), 1), TOKENS)
    visible = key_at <= token_at
    none = jnp.zeros((ROWS, HEAD), jnp.bfloat16)
    blank = jnp.zeros((TOKENS, 2 * HEAD), jnp.float32)
    blank_lanes = jnp.zeros((TOKENS, lanes), jnp.float32)

    def both(a, b, axis):
        return jnp.concatenate([a, b], axis=axis)

    def visit(i, _):
        a, b = order[2 * i], order[2 * i + 1]
        ga, gb = owners[2 * i], owners[2 * i + 1]

        def take(scratch, g):
            return scratch[:, g ^ spot[1]].reshape(-1, HEAD)

        def give(scratch, g, rows):
            scratch[place(g)] = rows.astype(jnp.bfloat16).reshape((4,) + scratch.shape[4:])

        def spread(rows):
            first = rows[pl.ds(pl.multiple_of(a * ROWS, ROWS), ROWS), :]
            second = rows[pl.ds(pl.multiple_of(b * ROWS, ROWS), ROWS), :]
            return both(both(first, none, 1), both(none, second, 1), 0)

        at_a = pl.ds(pl.multiple_of(a * TOKENS, TOKENS), TOKENS)
        at_b = pl.ds(pl.multiple_of(b * TOKENS, TOKENS), TOKENS)
        q, d = spread(q_rows), spread(d_rows)
        k = both(take(k_in, ga), take(k_in, gb), 1)
        v = both(take(v_in, ga), take(v_in, gb), 1)
        ko = both(both(own_k[at_a, :], own_k[at_b, :], 1), blank, 0).astype(jnp.bfloat16)
        vo = both(both(own_v[at_a, :], own_v[at_b, :], 1), blank, 0).astype(jnp.bfloat16)
        across, along = ((1,), (1,)), ((1,), (0,))
        s = dot(k, q, across)
        t = dot(v, d, across)
        so = jnp.where(visible, dot(ko, q, across)[:TOKENS], -1e30)
        to = dot(vo, d, across)[:TOKENS]
        top = jnp.maximum(jnp.max(s, axis=0, keepdims=True), jnp.max(so, axis=0, keepdims=True))
        e = jnp.exp2((s - top) * (SCALE * LOG2E))
        eo = jnp.exp2((so - top) * (SCALE * LOG2E))
        total = jnp.sum(e, axis=0, keepdims=True) + jnp.sum(eo, axis=0, keepdims=True)
        mixed = jnp.sum(e * t, axis=0, keepdims=True) + jnp.sum(eo * to, axis=0, keepdims=True)
        inverse = 1.0 / total
        delta = mixed * inverse
        p = e * inverse
        po = eo * inverse
        w = p.astype(jnp.bfloat16)
        ds = (p * (t - delta)).astype(jnp.bfloat16)
        wo = both(po, blank_lanes, 0).astype(jnp.bfloat16)
        dso = both(po * (to - delta), blank_lanes, 0).astype(jnp.bfloat16)
        dk = dot(ds, q, along) * SCALE
        dv = dot(w, d, along)
        dko = dot(dso, q, along)[:TOKENS] * SCALE
        dvo = dot(wo, d, along)[:TOKENS]
        down = ((0,), (0,))
        dq = (dot(ds, k, down) + dot(dso, ko, down)) * SCALE
        for at, rows in ((at_a, dq[:ROWS, :HEAD]), (at_b, dq[ROWS:, HEAD:])):
            dq_acc[at, :] = jnp.concatenate(
                [rows[h * TOKENS : (h + 1) * TOKENS] for h in range(PER_GROUP)], axis=1
            )
        drk_acc[at_a, :] = dko[:, :HEAD]
        drk_acc[at_b, :] = dko[:, HEAD:]
        drv_acc[at_a, :] = dvo[:, :HEAD]
        drv_acc[at_b, :] = dvo[:, HEAD:]
        shared = (ga == gb).astype(jnp.float32)
        give(dk_out, gb, dk[:, HEAD:])
        give(dv_out, gb, dv[:, HEAD:])
        give(dk_out, ga, dk[:, :HEAD] + shared * dk[:, HEAD:])
        give(dv_out, ga, dv[:, :HEAD] + shared * dv[:, HEAD:])
        return 0

    lax.fori_loop(0, responses // 2, visit, 0, unroll=2)
    stores = []
    for which in range(2):
        for group in range(2):
            for slot, block in enumerate(KEEP_SEND[which][group]):
                source = (dk_out, dv_out)[which]
                stores.append(
                    pltpu.make_async_copy(source.at[0, block], (here_k, here_v)[which][group].at[slot], left)
                )
                stores.append(pltpu.make_async_copy(source.at[1, block], there[group].at[which, slot], left))
    for store in stores:
        store.start()
    dq_ref[...] = dq_acc[...].astype(jnp.bfloat16)
    drk_ref[...] = drk_acc[...].astype(jnp.bfloat16)
    drv_ref[...] = drv_acc[...].astype(jnp.bfloat16)
    for store in stores:
        store.wait()


def attend(order, owners, spot, queries, cotangents, keys, values, gathered, head, gates):
    rows = queries.shape[0]
    prompts, _, length, _ = gathered.shape
    deep = prompts // 8
    inward = pltpu.VMEM((4, prompts, length, HEAD), jnp.bfloat16)
    positions = 4 * length
    wide = PER_GROUP * HEAD
    here = lambda shape: pl.BlockSpec(shape, lambda i, *_: (0, head))
    out = lambda shape: pl.BlockSpec(shape, lambda i, *_: (0, 0))
    far = pl.BlockSpec(memory_space=pl.ANY)
    outward = pltpu.VMEM((2, 4, 4, deep, length, HEAD), jnp.bfloat16)
    share = jax.ShapeDtypeStruct((2, 4, deep, length, HEAD), jnp.bfloat16)
    return pl.pallas_call(
        functools.partial(attend_kernel, FIRST[head], head),
        grid_spec=pltpu.PrefetchScalarGridSpec(
            num_scalar_prefetch=3,
            grid=(1,),
            in_specs=[here((rows, wide)), here((rows, wide)), here((rows, HEAD)), here((rows, HEAD))]
            + [far],
            out_specs=[out((rows, wide)), out((rows, HEAD)), out((rows, HEAD))] + [far] * 6,
            scratch_shapes=[
                pltpu.VMEM((rows * PER_GROUP, HEAD), jnp.bfloat16),
                pltpu.VMEM((rows * PER_GROUP, HEAD), jnp.bfloat16),
                pltpu.VMEM((rows, HEAD), jnp.float32),
                pltpu.VMEM((rows, HEAD), jnp.float32),
                pltpu.VMEM((rows, wide), jnp.float32),
                pltpu.VMEM((rows, HEAD), jnp.float32),
                pltpu.VMEM((rows, HEAD), jnp.float32),
                inward,
                inward,
                outward,
                outward,
                pltpu.SemaphoreType.DMA,
                pltpu.SemaphoreType.DMA,
            ],
        ),
        out_shape=[
            jax.ShapeDtypeStruct((rows, wide), jnp.bfloat16),
            jax.ShapeDtypeStruct((rows, HEAD), jnp.bfloat16),
            jax.ShapeDtypeStruct((rows, HEAD), jnp.bfloat16),
        ]
        + [share] * 4
        + [jax.ShapeDtypeStruct((2,) + share.shape, jnp.bfloat16)] * 2,
        compiler_params=pltpu.CompilerParams(vmem_limit_bytes=48 * 2**20),
        cost_estimate=pl.CostEstimate(
            flops=10 * rows * PER_GROUP * positions * HEAD,
            bytes_accessed=16 * prompts * positions * 2 * HEAD + 6 * rows * wide,
            transcendentals=rows * PER_GROUP * positions,
        ),
    )(after(order, *gates), owners, spot, queries, cotangents, keys, values, gathered)


def swap(array, axis, distance):
    count = lax.axis_size("wide") * lax.axis_size("narrow")
    flip = distance << BITS[axis]
    return lax.ppermute(array, ("wide", "narrow"), [(i, i ^ flip) for i in range(count)])


def other(axis):
    return "y" if axis == "x" else "x"


def after(value, *earlier):
    return lax.optimization_barrier((value, earlier))[0] if earlier else value


def sum_z(blocks):
    total = blocks[0].astype(jnp.float32)
    for step in range(1, 8):
        total = total + swap(blocks[step], "z", step).astype(jnp.float32)
    return total.astype(jnp.bfloat16)


def halve_near(kept, sent, way, axis):
    got = swap(sent, axis, NEAR_FAR[way][0])
    return kept[0] + got[0], kept[1] + got[1]


def halve_far(mine, other_sum, way, axis):
    return mine + swap(other_sum, axis, NEAR_FAR[way][1])


def pick(blocks, which):
    return jnp.stack([blocks[b] for b in which])


WAYS = (0, 1)


def body(queries, output_gradient, response_keys, response_values, prompt_key_rows, prompt_value_rows, prompt_index):
    here = lax.axis_index("wide").astype(jnp.int32)
    order, owners = paired_order(prompt_index[:, 0])
    owners = owners ^ here
    spot = jnp.stack([lax.axis_index("narrow").astype(jnp.int32), here])

    held = jnp.concatenate([prompt_key_rows[0], prompt_value_rows[0]], axis=1)
    gathered = lax.all_gather(held, ("wide", "narrow"), axis=0, tiled=True)
    gathered = gathered.reshape(-1, 4, held.shape[0], held.shape[1])

    def run(head, *gates):
        return attend(
            order, owners, spot, queries, output_gradient, response_keys, response_values, gathered, head, gates
        )

    def over_core(head, result):
        sent_there, kept_there = swap(result[8], "c", 1), swap(result[7], "c", 1)
        return {
            (way, head): (result[3 + 2 * way] + kept_there[way], result[4 + 2 * way] + sent_there[way])
            for way in WAYS
        }

    def near_first(sums):
        return {(w, h): halve_near(kept, sent, w, FIRST[h]) for (w, h), (kept, sent) in sums.items()}

    def far_first(halves, *gates):
        return {(w, h): halve_far(mine, after(far, *gates), w, FIRST[h]) for (w, h), (mine, far) in halves.items()}

    def second(mine, *gates):
        out = {}
        for (w, h), blocks in mine.items():
            blocks, axis = after(blocks, *gates), other(FIRST[h])
            kept, sent = pick(blocks, KEEP_SEND[w][0]), pick(blocks, KEEP_SEND[w][1])
            out[w, h] = halve_far(*halve_near(kept, sent, w, axis), w, axis)
        return out

    def flat(pairs):
        return [array for pair in pairs.values() for array in pair]

    results = {0: run(0)}
    results[1] = run(1, results[0][1])
    sums = over_core(0, results[0]) | over_core(1, results[1])
    results[2] = run(2, *flat(sums))
    halves = near_first(sums)
    results[3] = run(3, results[2][1], *flat(halves))
    mine = far_first(halves, results[2][1])
    total = second(mine, results[3][1])
    sums = over_core(2, results[2]) | over_core(3, results[3])
    total |= second(far_first(near_first(sums)))
    joined = jnp.concatenate([total[w, h] for w in WAYS for h in range(KEY_VALUE_HEADS)], axis=-1)
    summed = sum_z(joined)
    width = summed.shape[1] // 2
    key_sum, value_sum = summed[:, :width], summed[:, width:]
    dq, drk, drv = (jnp.concatenate([results[h][i] for h in range(KEY_VALUE_HEADS)], axis=1) for i in range(3))
    return dq, drk, drv, key_sum[None], value_sum[None]


def solution(mesh):
    spread = P(("wide", "narrow"), None)
    prompt = P("wide", "narrow", None)
    return jax.shard_map(
        body,
        mesh=mesh,
        in_specs=(spread, spread, spread, spread, prompt, prompt, spread),
        out_specs=(spread, spread, spread, prompt, prompt),
        check_vma=False,
    )
```

```python
import functools
import math

import jax
import jax.numpy as jnp
from jax import lax
from jax.experimental import pallas as pl
from jax.experimental.pallas import tpu as pltpu
from jax.sharding import PartitionSpec as P

QUERY_HEADS = 32
KEY_VALUE_HEADS = 4
PER_GROUP = QUERY_HEADS // KEY_VALUE_HEADS
HEAD = 128
TOKENS = 8
ROWS = PER_GROUP * TOKENS
SCALE = 1.0 / math.sqrt(HEAD)
LOG2E = math.log2(math.e)


def paired_order(targets):
    count = targets.shape[0]
    position = jnp.arange(count, dtype=jnp.int32)
    same = targets[:, None] == targets[None, :]
    before = position[None, :] < position[:, None]
    double = jnp.sum(same, axis=1) == 2
    first = jnp.logical_not(jnp.any(same & before, axis=1))
    head_of = jnp.sum(jnp.where(same & first[None, :], position[None, :], 0), axis=1)
    leads = double & first
    pair_rank = jnp.sum(leads[None, :] & (position[None, :] < head_of[:, None]), axis=1)
    single_rank = jnp.sum(jnp.logical_not(double)[None, :] & before, axis=1)
    slot = jnp.where(
        double,
        2 * pair_rank + jnp.logical_not(first).astype(jnp.int32),
        2 * jnp.sum(leads) + single_rank,
    )
    order = jnp.sum(jnp.where(slot[None, :] == position[:, None], position[None, :], 0), axis=1)
    owners = jnp.sum(jnp.where(slot[None, :] == position[:, None], targets[None, :], 0), axis=1)
    return order.astype(jnp.int32), owners.astype(jnp.int32)


def dot(left, right, contract):
    return lax.dot_general(left, right, (contract, ((), ())), preferred_element_type=jnp.float32)

KEEP_SEND = (((0, 3), (1, 2)), ((0, 1), (3, 2)))
NEAR_FAR = ((1, 3), (3, 1))
BITS = {"x": 0, "c": 2, "y": 3, "z": 5}
FIRST = ("x", "y", "x", "y")


def attend_kernel(first, head, order, owners, spot, q_ref, d_ref, rk_ref, rv_ref, gathered, *refs):
    dq_ref, drk_ref, drv_ref = refs[:3]
    here_k, here_v, there, refs = refs[3:5], refs[5:7], refs[7:9], refs[9:]
    q_rows, d_rows, own_k, own_v, dq_acc, drk_acc, drv_acc, k_in, v_in, dk_out, dv_out, arrived, left = refs
    responses = q_ref.shape[0] // TOKENS

    def place(g):
        core, y, z = g & 1, (g >> 1) & 3, g >> 3
        return (core, slice(None), y, z) if first == "x" else (core, y, slice(None), z)

    fetches = [
        pltpu.make_async_copy(
            gathered.at[:, spot[0] ^ block, :, pl.ds((KEY_VALUE_HEADS * which + head) * HEAD, HEAD)],
            (k_in, v_in)[which].at[block],
            arrived,
        )
        for which in range(2)
        for block in range(4)
    ]
    for fetch in fetches:
        fetch.start()

    def clear(g, _):
        for target in (dk_out, dv_out):
            for core in range(2):
                for block in range(4):
                    target[core, block, :, g] = jnp.zeros((4,) + target.shape[4:], target.dtype)
        return 0

    lax.fori_loop(0, dk_out.shape[3], clear, 0)
    own_k[...] = rk_ref[...].astype(jnp.float32)
    own_v[...] = rv_ref[...].astype(jnp.float32)

    def relay(p, _):
        lower = pl.multiple_of(p * 2 * TOKENS, 2 * TOKENS)
        for source, target in ((q_ref, q_rows), (d_ref, d_rows)):
            block = source[pl.ds(lower, 2 * TOKENS), :].astype(jnp.float32)
            stacked = jnp.concatenate(
                [
                    block[r * TOKENS : (r + 1) * TOKENS, h * HEAD : (h + 1) * HEAD]
                    for r in range(2)
                    for h in range(PER_GROUP)
                ],
                axis=0,
            )
            target[pl.ds(pl.multiple_of(p * 2 * ROWS, 2 * ROWS), 2 * ROWS), :] = stacked.astype(jnp.bfloat16)
        return 0

    lax.fori_loop(0, responses // 2, relay, 0)
    for fetch in fetches:
        fetch.wait()

    lanes = 2 * ROWS
    key_at = lax.broadcasted_iota(jnp.int32, (TOKENS, lanes), 0)
    token_at = lax.rem(lax.broadcasted_iota(jnp.int32, (TOKENS, lanes), 1), TOKENS)
    visible = key_at <= token_at
    none = jnp.zeros((ROWS, HEAD), jnp.bfloat16)
    blank = jnp.zeros((TOKENS, 2 * HEAD), jnp.float32)
    blank_lanes = jnp.zeros((TOKENS, lanes), jnp.float32)

    def both(a, b, axis):
        return jnp.concatenate([a, b], axis=axis)

    def visit(i, _):
        a, b = order[2 * i], order[2 * i + 1]
        ga, gb = owners[2 * i], owners[2 * i + 1]

        def take(scratch, g):
            return scratch[:, g ^ spot[1]].reshape(-1, HEAD)

        def give(scratch, g, rows):
            scratch[place(g)] = rows.astype(jnp.bfloat16).reshape((4,) + scratch.shape[4:])

        def spread(rows):
            first = rows[pl.ds(pl.multiple_of(a * ROWS, ROWS), ROWS), :]
            second = rows[pl.ds(pl.multiple_of(b * ROWS, ROWS), ROWS), :]
            return both(both(first, none, 1), both(none, second, 1), 0)

        at_a = pl.ds(pl.multiple_of(a * TOKENS, TOKENS), TOKENS)
        at_b = pl.ds(pl.multiple_of(b * TOKENS, TOKENS), TOKENS)
        q, d = spread(q_rows), spread(d_rows)
        k = both(take(k_in, ga), take(k_in, gb), 1)
        v = both(take(v_in, ga), take(v_in, gb), 1)
        ko = both(both(own_k[at_a, :], own_k[at_b, :], 1), blank, 0).astype(jnp.bfloat16)
        vo = both(both(own_v[at_a, :], own_v[at_b, :], 1), blank, 0).astype(jnp.bfloat16)
        across, along = ((1,), (1,)), ((1,), (0,))
        s = dot(k, q, across)
        t = dot(v, d, across)
        so = jnp.where(visible, dot(ko, q, across)[:TOKENS], -1e30)
        to = dot(vo, d, across)[:TOKENS]
        top = jnp.maximum(jnp.max(s, axis=0, keepdims=True), jnp.max(so, axis=0, keepdims=True))
        e = jnp.exp2((s - top) * (SCALE * LOG2E))
        eo = jnp.exp2((so - top) * (SCALE * LOG2E))
        total = jnp.sum(e, axis=0, keepdims=True) + jnp.sum(eo, axis=0, keepdims=True)
        mixed = jnp.sum(e * t, axis=0, keepdims=True) + jnp.sum(eo * to, axis=0, keepdims=True)
        inverse = 1.0 / total
        delta = mixed * inverse
        p = e * inverse
        po = eo * inverse
        w = p.astype(jnp.bfloat16)
        ds = (p * (t - delta)).astype(jnp.bfloat16)
        wo = both(po, blank_lanes, 0).astype(jnp.bfloat16)
        dso = both(po * (to - delta), blank_lanes, 0).astype(jnp.bfloat16)
        dk = dot(ds, q, along) * SCALE
        dv = dot(w, d, along)
        dko = dot(dso, q, along)[:TOKENS] * SCALE
        dvo = dot(wo, d, along)[:TOKENS]
        down = ((0,), (0,))
        dq = (dot(ds, k, down) + dot(dso, ko, down)) * SCALE
        for at, rows in ((at_a, dq[:ROWS, :HEAD]), (at_b, dq[ROWS:, HEAD:])):
            dq_acc[at, :] = jnp.concatenate(
                [rows[h * TOKENS : (h + 1) * TOKENS] for h in range(PER_GROUP)], axis=1
            )
        drk_acc[at_a, :] = dko[:, :HEAD]
        drk_acc[at_b, :] = dko[:, HEAD:]
        drv_acc[at_a, :] = dvo[:, :HEAD]
        drv_acc[at_b, :] = dvo[:, HEAD:]
        shared = (ga == gb).astype(jnp.float32)
        give(dk_out, gb, dk[:, HEAD:])
        give(dv_out, gb, dv[:, HEAD:])
        give(dk_out, ga, dk[:, :HEAD] + shared * dk[:, HEAD:])
        give(dv_out, ga, dv[:, :HEAD] + shared * dv[:, HEAD:])
        return 0

    lax.fori_loop(0, responses // 2, visit, 0, unroll=2)
    stores = []
    for which in range(2):
        for group in range(2):
            for slot, block in enumerate(KEEP_SEND[which][group]):
                source = (dk_out, dv_out)[which]
                stores.append(
                    pltpu.make_async_copy(source.at[0, block], (here_k, here_v)[which][group].at[slot], left)
                )
                stores.append(pltpu.make_async_copy(source.at[1, block], there[group].at[which, slot], left))
    for store in stores:
        store.start()
    dq_ref[...] = dq_acc[...].astype(jnp.bfloat16)
    drk_ref[...] = drk_acc[...].astype(jnp.bfloat16)
    drv_ref[...] = drv_acc[...].astype(jnp.bfloat16)
    for store in stores:
        store.wait()


def attend(order, owners, spot, queries, cotangents, keys, values, gathered, head, gates):
    rows = queries.shape[0]
    prompts, _, length, _ = gathered.shape
    deep = prompts // 8
    inward = pltpu.VMEM((4, prompts, length, HEAD), jnp.bfloat16)
    positions = 4 * length
    wide = PER_GROUP * HEAD
    here = lambda shape: pl.BlockSpec(shape, lambda i, *_: (0, head))
    out = lambda shape: pl.BlockSpec(shape, lambda i, *_: (0, 0))
    far = pl.BlockSpec(memory_space=pl.ANY)
    outward = pltpu.VMEM((2, 4, 4, deep, length, HEAD), jnp.bfloat16)
    share = jax.ShapeDtypeStruct((2, 4, deep, length, HEAD), jnp.bfloat16)
    return pl.pallas_call(
        functools.partial(attend_kernel, FIRST[head], head),
        grid_spec=pltpu.PrefetchScalarGridSpec(
            num_scalar_prefetch=3,
            grid=(1,),
            in_specs=[here((rows, wide)), here((rows, wide)), here((rows, HEAD)), here((rows, HEAD))]
            + [far],
            out_specs=[out((rows, wide)), out((rows, HEAD)), out((rows, HEAD))] + [far] * 6,
            scratch_shapes=[
                pltpu.VMEM((rows * PER_GROUP, HEAD), jnp.bfloat16),
                pltpu.VMEM((rows * PER_GROUP, HEAD), jnp.bfloat16),
                pltpu.VMEM((rows, HEAD), jnp.float32),
                pltpu.VMEM((rows, HEAD), jnp.float32),
                pltpu.VMEM((rows, wide), jnp.float32),
                pltpu.VMEM((rows, HEAD), jnp.float32),
                pltpu.VMEM((rows, HEAD), jnp.float32),
                inward,
                inward,
                outward,
                outward,
                pltpu.SemaphoreType.DMA,
                pltpu.SemaphoreType.DMA,
            ],
        ),
        out_shape=[
            jax.ShapeDtypeStruct((rows, wide), jnp.bfloat16),
            jax.ShapeDtypeStruct((rows, HEAD), jnp.bfloat16),
            jax.ShapeDtypeStruct((rows, HEAD), jnp.bfloat16),
        ]
        + [share] * 4
        + [jax.ShapeDtypeStruct((2,) + share.shape, jnp.bfloat16)] * 2,
        compiler_params=pltpu.CompilerParams(vmem_limit_bytes=48 * 2**20),
        cost_estimate=pl.CostEstimate(
            flops=10 * rows * PER_GROUP * positions * HEAD,
            bytes_accessed=16 * prompts * positions * 2 * HEAD + 6 * rows * wide,
            transcendentals=rows * PER_GROUP * positions,
        ),
    )(after(order, *gates), owners, spot, queries, cotangents, keys, values, gathered)


def swap(array, axis, distance):
    count = lax.axis_size("wide") * lax.axis_size("narrow")
    flip = distance << BITS[axis]
    return lax.ppermute(array, ("wide", "narrow"), [(i, i ^ flip) for i in range(count)])


def other(axis):
    return "y" if axis == "x" else "x"


def after(value, *earlier):
    return lax.optimization_barrier((value, earlier))[0] if earlier else value


def sum_z(blocks):
    total = blocks[0].astype(jnp.float32)
    for step in range(1, 8):
        total = total + swap(blocks[step], "z", step).astype(jnp.float32)
    return total.astype(jnp.bfloat16)


def halve_near(kept, sent, way, axis):
    got = swap(sent, axis, NEAR_FAR[way][0])
    return kept[0] + got[0], kept[1] + got[1]


def halve_far(mine, other_sum, way, axis):
    return mine + swap(other_sum, axis, NEAR_FAR[way][1])


def pick(blocks, which):
    return jnp.stack([blocks[b] for b in which])


WAYS = (0, 1)


def body(queries, output_gradient, response_keys, response_values, prompt_key_rows, prompt_value_rows, prompt_index):
    here = lax.axis_index("wide").astype(jnp.int32)
    order, owners = paired_order(prompt_index[:, 0])
    owners = owners ^ here
    spot = jnp.stack([lax.axis_index("narrow").astype(jnp.int32), here])

    held = jnp.concatenate([prompt_key_rows[0], prompt_value_rows[0]], axis=1)
    gathered = lax.all_gather(held, ("wide", "narrow"), axis=0, tiled=True)
    gathered = gathered.reshape(-1, 4, held.shape[0], held.shape[1])

    def run(head, *gates):
        return attend(
            order, owners, spot, queries, output_gradient, response_keys, response_values, gathered, head, gates
        )

    results = {0: run(0)}
    results[1] = run(1, results[0][1])

    def over_core(heads, slot):
        there = {h: swap(results[h][7 + slot], "c", 1) for h in heads}
        return {(w, h): results[h][3 + 2 * w + slot] + there[h][w] for h in heads for w in WAYS}

    def near_first(sent):
        return {(w, h): swap(array, FIRST[h], NEAR_FAR[w][0]) for (w, h), array in sent.items()}

    def far_first(kept, got, *gates):
        out = {}
        for (w, h), mine in kept.items():
            far = after(mine[1] + got[w, h][1], *gates)
            out[w, h] = mine[0] + got[w, h][0] + swap(far, FIRST[h], NEAR_FAR[w][1])
        return out

    sent = over_core((0, 1), 1)
    got = near_first(sent)
    kept = over_core((0, 1), 0)
    results[2] = run(2, *sent.values())
    results[3] = run(3, results[2][1])
    mine = far_first(kept, got, results[3][1])
    sent = over_core((2, 3), 1)
    got = near_first(sent)
    kept = over_core((2, 3), 0)
    mine |= far_first(kept, got)
    total = {}
    for w in WAYS:
        for axis in ("x", "y"):
            heads = [h for h in range(KEY_VALUE_HEADS) if other(FIRST[h]) == axis]
            blocks = jnp.concatenate([mine[w, h] for h in heads], axis=-1)
            pairs = pick(blocks, KEEP_SEND[w][0]), pick(blocks, KEEP_SEND[w][1])
            result = halve_far(*halve_near(*pairs, w, axis), w, axis)
            for i, h in enumerate(heads):
                total[w, h] = result[..., i * HEAD : (i + 1) * HEAD]
    joined = jnp.concatenate([total[w, h] for w in WAYS for h in range(KEY_VALUE_HEADS)], axis=-1)
    summed = sum_z(joined)
    width = summed.shape[1] // 2
    key_sum, value_sum = summed[:, :width], summed[:, width:]
    dq, drk, drv = (jnp.concatenate([results[h][i] for h in range(KEY_VALUE_HEADS)], axis=1) for i in range(3))
    return dq, drk, drv, key_sum[None], value_sum[None]


def solution(mesh):
    spread = P(("wide", "narrow"), None)
    prompt = P("wide", "narrow", None)
    return jax.shard_map(
        body,
        mesh=mesh,
        in_specs=(spread, spread, spread, spread, prompt, prompt, spread),
        out_specs=(spread, spread, spread, prompt, prompt),
        check_vma=False,
    )
```

```python
import functools
import math

import jax
import jax.numpy as jnp
from jax import lax
from jax.experimental import pallas as pl
from jax.experimental.pallas import tpu as pltpu
from jax.sharding import PartitionSpec as P

QUERY_HEADS = 32
KEY_VALUE_HEADS = 4
PER_GROUP = QUERY_HEADS // KEY_VALUE_HEADS
HEAD = 128
TOKENS = 8
ROWS = PER_GROUP * TOKENS
SCALE = 1.0 / math.sqrt(HEAD)
LOG2E = math.log2(math.e)


def paired_order(targets):
    count = targets.shape[0]
    position = jnp.arange(count, dtype=jnp.int32)
    same = targets[:, None] == targets[None, :]
    before = position[None, :] < position[:, None]
    double = jnp.sum(same, axis=1) == 2
    first = jnp.logical_not(jnp.any(same & before, axis=1))
    head_of = jnp.sum(jnp.where(same & first[None, :], position[None, :], 0), axis=1)
    leads = double & first
    pair_rank = jnp.sum(leads[None, :] & (position[None, :] < head_of[:, None]), axis=1)
    single_rank = jnp.sum(jnp.logical_not(double)[None, :] & before, axis=1)
    slot = jnp.where(
        double,
        2 * pair_rank + jnp.logical_not(first).astype(jnp.int32),
        2 * jnp.sum(leads) + single_rank,
    )
    order = jnp.sum(jnp.where(slot[None, :] == position[:, None], position[None, :], 0), axis=1)
    owners = jnp.sum(jnp.where(slot[None, :] == position[:, None], targets[None, :], 0), axis=1)
    return order.astype(jnp.int32), owners.astype(jnp.int32)


def dot(left, right, contract):
    return lax.dot_general(left, right, (contract, ((), ())), preferred_element_type=jnp.float32)

KEEP_SEND = (((0, 3), (1, 2)), ((0, 1), (3, 2)))
NEAR_FAR = ((1, 3), (3, 1))
BITS = {"x": 0, "c": 2, "y": 3, "z": 5}
FIRST = ("x", "y", "x", "y")


def attend_kernel(first, head, order, owners, spot, q_ref, d_ref, rk_ref, rv_ref, gathered, *refs):
    dq_ref, drk_ref, drv_ref = refs[:3]
    here_k, here_v, there, refs = refs[3:5], refs[5:7], refs[7:9], refs[9:]
    q_rows, d_rows, own_k, own_v, dq_acc, drk_acc, drv_acc, k_in, v_in, dk_out, dv_out, arrived, left = refs
    responses = q_ref.shape[0] // TOKENS

    def place(g):
        core, y, z = g & 1, (g >> 1) & 3, g >> 3
        return (core, slice(None), y, z) if first == "x" else (core, y, slice(None), z)

    fetches = [
        pltpu.make_async_copy(
            gathered.at[:, spot[0] ^ block, :, pl.ds((KEY_VALUE_HEADS * which + head) * HEAD, HEAD)],
            (k_in, v_in)[which].at[block],
            arrived,
        )
        for which in range(2)
        for block in range(4)
    ]
    for fetch in fetches:
        fetch.start()

    def clear(g, _):
        for target in (dk_out, dv_out):
            for core in range(2):
                for block in range(4):
                    target[core, block, :, g] = jnp.zeros((4,) + target.shape[4:], target.dtype)
        return 0

    lax.fori_loop(0, dk_out.shape[3], clear, 0)
    own_k[...] = rk_ref[...].astype(jnp.float32)
    own_v[...] = rv_ref[...].astype(jnp.float32)

    def relay(p, _):
        lower = pl.multiple_of(p * 2 * TOKENS, 2 * TOKENS)
        for source, target in ((q_ref, q_rows), (d_ref, d_rows)):
            block = source[pl.ds(lower, 2 * TOKENS), :].astype(jnp.float32)
            stacked = jnp.concatenate(
                [
                    block[r * TOKENS : (r + 1) * TOKENS, h * HEAD : (h + 1) * HEAD]
                    for r in range(2)
                    for h in range(PER_GROUP)
                ],
                axis=0,
            )
            target[pl.ds(pl.multiple_of(p * 2 * ROWS, 2 * ROWS), 2 * ROWS), :] = stacked.astype(jnp.bfloat16)
        return 0

    lax.fori_loop(0, responses // 2, relay, 0)
    for fetch in fetches:
        fetch.wait()

    lanes = 2 * ROWS
    key_at = lax.broadcasted_iota(jnp.int32, (TOKENS, lanes), 0)
    token_at = lax.rem(lax.broadcasted_iota(jnp.int32, (TOKENS, lanes), 1), TOKENS)
    visible = key_at <= token_at
    none = jnp.zeros((ROWS, HEAD), jnp.bfloat16)
    blank = jnp.zeros((TOKENS, 2 * HEAD), jnp.float32)
    blank_lanes = jnp.zeros((TOKENS, lanes), jnp.float32)

    def both(a, b, axis):
        return jnp.concatenate([a, b], axis=axis)

    def visit(i, _):
        a, b = order[2 * i], order[2 * i + 1]
        ga, gb = owners[2 * i], owners[2 * i + 1]

        def take(scratch, g):
            return scratch[:, g ^ spot[1]].reshape(-1, HEAD)

        def give(scratch, g, rows):
            scratch[place(g)] = rows.astype(jnp.bfloat16).reshape((4,) + scratch.shape[4:])

        def spread(rows):
            first = rows[pl.ds(pl.multiple_of(a * ROWS, ROWS), ROWS), :]
            second = rows[pl.ds(pl.multiple_of(b * ROWS, ROWS), ROWS), :]
            return both(both(first, none, 1), both(none, second, 1), 0)

        at_a = pl.ds(pl.multiple_of(a * TOKENS, TOKENS), TOKENS)
        at_b = pl.ds(pl.multiple_of(b * TOKENS, TOKENS), TOKENS)
        q, d = spread(q_rows), spread(d_rows)
        k = both(take(k_in, ga), take(k_in, gb), 1)
        v = both(take(v_in, ga), take(v_in, gb), 1)
        ko = both(both(own_k[at_a, :], own_k[at_b, :], 1), blank, 0).astype(jnp.bfloat16)
        vo = both(both(own_v[at_a, :], own_v[at_b, :], 1), blank, 0).astype(jnp.bfloat16)
        across, along = ((1,), (1,)), ((1,), (0,))
        s = dot(k, q, across)
        t = dot(v, d, across)
        so = jnp.where(visible, dot(ko, q, across)[:TOKENS], -1e30)
        to = dot(vo, d, across)[:TOKENS]
        top = jnp.maximum(jnp.max(s, axis=0, keepdims=True), jnp.max(so, axis=0, keepdims=True))
        e = jnp.exp2((s - top) * (SCALE * LOG2E))
        eo = jnp.exp2((so - top) * (SCALE * LOG2E))
        total = jnp.sum(e, axis=0, keepdims=True) + jnp.sum(eo, axis=0, keepdims=True)
        mixed = jnp.sum(e * t, axis=0, keepdims=True) + jnp.sum(eo * to, axis=0, keepdims=True)
        inverse = 1.0 / total
        delta = mixed * inverse
        p = e * inverse
        po = eo * inverse
        w = p.astype(jnp.bfloat16)
        ds = (p * (t - delta)).astype(jnp.bfloat16)
        wo = both(po, blank_lanes, 0).astype(jnp.bfloat16)
        dso = both(po * (to - delta), blank_lanes, 0).astype(jnp.bfloat16)
        dk = dot(ds, q, along) * SCALE
        dv = dot(w, d, along)
        dko = dot(dso, q, along)[:TOKENS] * SCALE
        dvo = dot(wo, d, along)[:TOKENS]
        down = ((0,), (0,))
        dq = (dot(ds, k, down) + dot(dso, ko, down)) * SCALE
        for at, rows in ((at_a, dq[:ROWS, :HEAD]), (at_b, dq[ROWS:, HEAD:])):
            dq_acc[at, :] = jnp.concatenate(
                [rows[h * TOKENS : (h + 1) * TOKENS] for h in range(PER_GROUP)], axis=1
            )
        drk_acc[at_a, :] = dko[:, :HEAD]
        drk_acc[at_b, :] = dko[:, HEAD:]
        drv_acc[at_a, :] = dvo[:, :HEAD]
        drv_acc[at_b, :] = dvo[:, HEAD:]
        shared = (ga == gb).astype(jnp.float32)
        give(dk_out, gb, dk[:, HEAD:])
        give(dv_out, gb, dv[:, HEAD:])
        give(dk_out, ga, dk[:, :HEAD] + shared * dk[:, HEAD:])
        give(dv_out, ga, dv[:, :HEAD] + shared * dv[:, HEAD:])
        return 0

    lax.fori_loop(0, responses // 2, visit, 0, unroll=3)
    stores = []
    for which in range(2):
        for group in range(2):
            for slot, block in enumerate(KEEP_SEND[which][group]):
                source = (dk_out, dv_out)[which]
                stores.append(
                    pltpu.make_async_copy(source.at[0, block], (here_k, here_v)[which][group].at[slot], left)
                )
                stores.append(pltpu.make_async_copy(source.at[1, block], there[group].at[which, slot], left))
    for store in stores:
        store.start()
    dq_ref[...] = dq_acc[...].astype(jnp.bfloat16)
    drk_ref[...] = drk_acc[...].astype(jnp.bfloat16)
    drv_ref[...] = drv_acc[...].astype(jnp.bfloat16)
    for store in stores:
        store.wait()


def attend(order, owners, spot, queries, cotangents, keys, values, gathered, head, gates):
    rows = queries.shape[0]
    prompts, _, length, _ = gathered.shape
    deep = prompts // 8
    inward = pltpu.VMEM((4, prompts, length, HEAD), jnp.bfloat16)
    positions = 4 * length
    wide = PER_GROUP * HEAD
    here = lambda shape: pl.BlockSpec(shape, lambda i, *_: (0, head))
    out = lambda shape: pl.BlockSpec(shape, lambda i, *_: (0, 0))
    far = pl.BlockSpec(memory_space=pl.ANY)
    outward = pltpu.VMEM((2, 4, 4, deep, length, HEAD), jnp.bfloat16)
    share = jax.ShapeDtypeStruct((2, 4, deep, length, HEAD), jnp.bfloat16)
    return pl.pallas_call(
        functools.partial(attend_kernel, FIRST[head], head),
        grid_spec=pltpu.PrefetchScalarGridSpec(
            num_scalar_prefetch=3,
            grid=(1,),
            in_specs=[here((rows, wide)), here((rows, wide)), here((rows, HEAD)), here((rows, HEAD))]
            + [far],
            out_specs=[out((rows, wide)), out((rows, HEAD)), out((rows, HEAD))] + [far] * 6,
            scratch_shapes=[
                pltpu.VMEM((rows * PER_GROUP, HEAD), jnp.bfloat16),
                pltpu.VMEM((rows * PER_GROUP, HEAD), jnp.bfloat16),
                pltpu.VMEM((rows, HEAD), jnp.float32),
                pltpu.VMEM((rows, HEAD), jnp.float32),
                pltpu.VMEM((rows, wide), jnp.float32),
                pltpu.VMEM((rows, HEAD), jnp.float32),
                pltpu.VMEM((rows, HEAD), jnp.float32),
                inward,
                inward,
                outward,
                outward,
                pltpu.SemaphoreType.DMA,
                pltpu.SemaphoreType.DMA,
            ],
        ),
        out_shape=[
            jax.ShapeDtypeStruct((rows, wide), jnp.bfloat16),
            jax.ShapeDtypeStruct((rows, HEAD), jnp.bfloat16),
            jax.ShapeDtypeStruct((rows, HEAD), jnp.bfloat16),
        ]
        + [share] * 4
        + [jax.ShapeDtypeStruct((2,) + share.shape, jnp.bfloat16)] * 2,
        compiler_params=pltpu.CompilerParams(vmem_limit_bytes=48 * 2**20),
        cost_estimate=pl.CostEstimate(
            flops=10 * rows * PER_GROUP * positions * HEAD,
            bytes_accessed=16 * prompts * positions * 2 * HEAD + 6 * rows * wide,
            transcendentals=rows * PER_GROUP * positions,
        ),
    )(after(order, *gates), owners, spot, queries, cotangents, keys, values, gathered)


def swap(array, axis, distance):
    count = lax.axis_size("wide") * lax.axis_size("narrow")
    flip = distance << BITS[axis]
    return lax.ppermute(array, ("wide", "narrow"), [(i, i ^ flip) for i in range(count)])


def other(axis):
    return "y" if axis == "x" else "x"


def after(value, *earlier):
    return lax.optimization_barrier((value, earlier))[0] if earlier else value


def sum_z(blocks):
    even, odd = blocks[0::2], blocks[1::2]
    pairs = even + swap(odd, "z", 1)
    total = pairs[0].astype(jnp.float32)
    for step in range(1, 4):
        total = total + swap(pairs[step], "z", 2 * step).astype(jnp.float32)
    return total.astype(jnp.bfloat16)


def halve_near(kept, sent, way, axis):
    got = swap(sent, axis, NEAR_FAR[way][0])
    return kept[0] + got[0], kept[1] + got[1]


def halve_far(mine, other_sum, way, axis):
    return mine + swap(other_sum, axis, NEAR_FAR[way][1])


def pick(blocks, which):
    return jnp.stack([blocks[b] for b in which])


WAYS = (0, 1)


def body(queries, output_gradient, response_keys, response_values, prompt_key_rows, prompt_value_rows, prompt_index):
    here = lax.axis_index("wide").astype(jnp.int32)
    order, owners = paired_order(prompt_index[:, 0])
    owners = owners ^ here
    spot = jnp.stack([lax.axis_index("narrow").astype(jnp.int32), here])

    held = jnp.concatenate([prompt_key_rows[0], prompt_value_rows[0]], axis=1)
    gathered = lax.all_gather(held, ("wide", "narrow"), axis=0, tiled=True)
    gathered = gathered.reshape(-1, 4, held.shape[0], held.shape[1])

    def run(head, *gates):
        return attend(
            order, owners, spot, queries, output_gradient, response_keys, response_values, gathered, head, gates
        )

    results = {0: run(0)}
    results[1] = run(1, results[0][1])

    def over_core(heads, slot, *gates):
        there = {h: swap(after(results[h][7 + slot], *gates), "c", 1) for h in heads}
        return {(w, h): results[h][3 + 2 * w + slot] + there[h][w] for h in heads for w in WAYS}

    def near_first(sent):
        return {(w, h): swap(array, FIRST[h], NEAR_FAR[w][0]) for (w, h), array in sent.items()}

    def far_first(kept, got, *gates):
        out = {}
        for (w, h), mine in kept.items():
            far = after(mine[1] + got[w, h][1], *gates)
            out[w, h] = mine[0] + got[w, h][0] + swap(far, FIRST[h], NEAR_FAR[w][1])
        return out

    sent = over_core((0, 1), 1)
    got = near_first(sent)
    kept = over_core((0, 1), 0)
    results[2] = run(2, *sent.values())
    results[3] = run(3, results[2][1])
    mine = far_first(kept, got, results[3][1])
    sent = over_core((2, 3), 1, *mine.values())
    got = near_first(sent)
    kept = over_core((2, 3), 0, *sent.values())
    mine |= far_first(kept, got)
    total = {}
    for w in WAYS:
        for axis in ("x", "y"):
            heads = [h for h in range(KEY_VALUE_HEADS) if other(FIRST[h]) == axis]
            blocks = jnp.concatenate([mine[w, h] for h in heads], axis=-1)
            pairs = pick(blocks, KEEP_SEND[w][0]), pick(blocks, KEEP_SEND[w][1])
            result = halve_far(*halve_near(*pairs, w, axis), w, axis)
            for i, h in enumerate(heads):
                total[w, h] = result[..., i * HEAD : (i + 1) * HEAD]
    joined = jnp.concatenate([total[w, h] for w in WAYS for h in range(KEY_VALUE_HEADS)], axis=-1)
    summed = sum_z(joined)
    width = summed.shape[1] // 2
    key_sum, value_sum = summed[:, :width], summed[:, width:]
    dq, drk, drv = (jnp.concatenate([results[h][i] for h in range(KEY_VALUE_HEADS)], axis=1) for i in range(3))
    return dq, drk, drv, key_sum[None], value_sum[None]


def solution(mesh):
    spread = P(("wide", "narrow"), None)
    prompt = P("wide", "narrow", None)
    return jax.shard_map(
        body,
        mesh=mesh,
        in_specs=(spread, spread, spread, spread, prompt, prompt, spread),
        out_specs=(spread, spread, spread, prompt, prompt),
        check_vma=False,
    )
```

```python
import functools
import math

import jax
import jax.numpy as jnp
from jax import lax
from jax.experimental import pallas as pl
from jax.experimental.pallas import tpu as pltpu
from jax.sharding import PartitionSpec as P

QUERY_HEADS = 32
KEY_VALUE_HEADS = 4
PER_GROUP = QUERY_HEADS // KEY_VALUE_HEADS
HEAD = 128
TOKENS = 8
ROWS = PER_GROUP * TOKENS
SCALE = 1.0 / math.sqrt(HEAD)
LOG2E = math.log2(math.e)


def paired_order(targets):
    count = targets.shape[0]
    position = jnp.arange(count, dtype=jnp.int32)
    same = targets[:, None] == targets[None, :]
    before = position[None, :] < position[:, None]
    double = jnp.sum(same, axis=1) == 2
    first = jnp.logical_not(jnp.any(same & before, axis=1))
    head_of = jnp.sum(jnp.where(same & first[None, :], position[None, :], 0), axis=1)
    leads = double & first
    pair_rank = jnp.sum(leads[None, :] & (position[None, :] < head_of[:, None]), axis=1)
    single_rank = jnp.sum(jnp.logical_not(double)[None, :] & before, axis=1)
    slot = jnp.where(
        double,
        2 * pair_rank + jnp.logical_not(first).astype(jnp.int32),
        2 * jnp.sum(leads) + single_rank,
    )
    order = jnp.sum(jnp.where(slot[None, :] == position[:, None], position[None, :], 0), axis=1)
    owners = jnp.sum(jnp.where(slot[None, :] == position[:, None], targets[None, :], 0), axis=1)
    return order.astype(jnp.int32), owners.astype(jnp.int32)


def dot(left, right, contract):
    return lax.dot_general(left, right, (contract, ((), ())), preferred_element_type=jnp.float32)

KEEP_SEND = (((0, 3), (1, 2)), ((0, 1), (3, 2)))
NEAR_FAR = ((1, 3), (3, 1))
BITS = {"x": 0, "c": 2, "y": 3, "z": 5}
FIRST = ("x", "y", "x", "y")


def attend_kernel(first, head, joint, order, owners, spot, q_ref, d_ref, rk_ref, rv_ref, gathered, *refs):
    dq_ref, drk_ref, drv_ref = refs[:3]
    here_k, here_v, refs = refs[3:5], refs[5:7], refs[7:]
    there, refs = ((refs[0].at[0], refs[0].at[1]), refs[1:]) if joint else (refs[:2], refs[2:])
    q_rows, d_rows, own_k, own_v, dq_acc, drk_acc, drv_acc, k_in, v_in, dk_out, dv_out, arrived, left = refs
    responses = q_ref.shape[0] // TOKENS

    def place(g):
        core, y, z = g & 1, (g >> 1) & 3, g >> 3
        return (core, slice(None), y, z) if first == "x" else (core, y, slice(None), z)

    fetches = [
        pltpu.make_async_copy(
            gathered.at[:, spot[0] ^ block, :, pl.ds((KEY_VALUE_HEADS * which + head) * HEAD, HEAD)],
            (k_in, v_in)[which].at[block],
            arrived,
        )
        for which in range(2)
        for block in range(4)
    ]
    for fetch in fetches:
        fetch.start()

    def clear(g, _):
        for target in (dk_out, dv_out):
            for core in range(2):
                for block in range(4):
                    target[core, block, :, g] = jnp.zeros((4,) + target.shape[4:], target.dtype)
        return 0

    lax.fori_loop(0, dk_out.shape[3], clear, 0)
    own_k[...] = rk_ref[...].astype(jnp.float32)
    own_v[...] = rv_ref[...].astype(jnp.float32)

    def relay(p, _):
        lower = pl.multiple_of(p * 2 * TOKENS, 2 * TOKENS)
        for source, target in ((q_ref, q_rows), (d_ref, d_rows)):
            block = source[pl.ds(lower, 2 * TOKENS), :].astype(jnp.float32)
            stacked = jnp.concatenate(
                [
                    block[r * TOKENS : (r + 1) * TOKENS, h * HEAD : (h + 1) * HEAD]
                    for r in range(2)
                    for h in range(PER_GROUP)
                ],
                axis=0,
            )
            target[pl.ds(pl.multiple_of(p * 2 * ROWS, 2 * ROWS), 2 * ROWS), :] = stacked.astype(jnp.bfloat16)
        return 0

    lax.fori_loop(0, responses // 2, relay, 0)
    for fetch in fetches:
        fetch.wait()

    lanes = 2 * ROWS
    key_at = lax.broadcasted_iota(jnp.int32, (TOKENS, lanes), 0)
    token_at = lax.rem(lax.broadcasted_iota(jnp.int32, (TOKENS, lanes), 1), TOKENS)
    visible = key_at <= token_at
    none = jnp.zeros((ROWS, HEAD), jnp.bfloat16)
    blank = jnp.zeros((TOKENS, 2 * HEAD), jnp.float32)
    blank_lanes = jnp.zeros((TOKENS, lanes), jnp.float32)

    def both(a, b, axis):
        return jnp.concatenate([a, b], axis=axis)

    def visit(i, _):
        a, b = order[2 * i], order[2 * i + 1]
        ga, gb = owners[2 * i], owners[2 * i + 1]

        def take(scratch, g):
            return scratch[:, g ^ spot[1]].reshape(-1, HEAD)

        def give(scratch, g, rows):
            scratch[place(g)] = rows.astype(jnp.bfloat16).reshape((4,) + scratch.shape[4:])

        def spread(rows):
            first = rows[pl.ds(pl.multiple_of(a * ROWS, ROWS), ROWS), :]
            second = rows[pl.ds(pl.multiple_of(b * ROWS, ROWS), ROWS), :]
            return both(both(first, none, 1), both(none, second, 1), 0)

        at_a = pl.ds(pl.multiple_of(a * TOKENS, TOKENS), TOKENS)
        at_b = pl.ds(pl.multiple_of(b * TOKENS, TOKENS), TOKENS)
        q, d = spread(q_rows), spread(d_rows)
        k = both(take(k_in, ga), take(k_in, gb), 1)
        v = both(take(v_in, ga), take(v_in, gb), 1)
        ko = both(both(own_k[at_a, :], own_k[at_b, :], 1), blank, 0).astype(jnp.bfloat16)
        vo = both(both(own_v[at_a, :], own_v[at_b, :], 1), blank, 0).astype(jnp.bfloat16)
        across, along = ((1,), (1,)), ((1,), (0,))
        s = dot(k, q, across)
        t = dot(v, d, across)
        so = jnp.where(visible, dot(ko, q, across)[:TOKENS], -1e30)
        to = dot(vo, d, across)[:TOKENS]
        top = jnp.maximum(jnp.max(s, axis=0, keepdims=True), jnp.max(so, axis=0, keepdims=True))
        e = jnp.exp2((s - top) * (SCALE * LOG2E))
        eo = jnp.exp2((so - top) * (SCALE * LOG2E))
        total = jnp.sum(e, axis=0, keepdims=True) + jnp.sum(eo, axis=0, keepdims=True)
        mixed = jnp.sum(e * t, axis=0, keepdims=True) + jnp.sum(eo * to, axis=0, keepdims=True)
        inverse = 1.0 / total
        delta = mixed * inverse
        p = e * inverse
        po = eo * inverse
        w = p.astype(jnp.bfloat16)
        ds = (p * (t - delta)).astype(jnp.bfloat16)
        wo = both(po, blank_lanes, 0).astype(jnp.bfloat16)
        dso = both(po * (to - delta), blank_lanes, 0).astype(jnp.bfloat16)
        dk = dot(ds, q, along) * SCALE
        dv = dot(w, d, along)
        dko = dot(dso, q, along)[:TOKENS] * SCALE
        dvo = dot(wo, d, along)[:TOKENS]
        down = ((0,), (0,))
        dq = (dot(ds, k, down) + dot(dso, ko, down)) * SCALE
        for at, rows in ((at_a, dq[:ROWS, :HEAD]), (at_b, dq[ROWS:, HEAD:])):
            dq_acc[at, :] = jnp.concatenate(
                [rows[h * TOKENS : (h + 1) * TOKENS] for h in range(PER_GROUP)], axis=1
            )
        drk_acc[at_a, :] = dko[:, :HEAD]
        drk_acc[at_b, :] = dko[:, HEAD:]
        drv_acc[at_a, :] = dvo[:, :HEAD]
        drv_acc[at_b, :] = dvo[:, HEAD:]
        shared = (ga == gb).astype(jnp.float32)
        give(dk_out, gb, dk[:, HEAD:])
        give(dv_out, gb, dv[:, HEAD:])
        give(dk_out, ga, dk[:, :HEAD] + shared * dk[:, HEAD:])
        give(dv_out, ga, dv[:, :HEAD] + shared * dv[:, HEAD:])
        return 0

    lax.fori_loop(0, responses // 2, visit, 0, unroll=3)
    stores = []
    for which in range(2):
        for group in range(2):
            for slot, block in enumerate(KEEP_SEND[which][group]):
                source = (dk_out, dv_out)[which]
                stores.append(
                    pltpu.make_async_copy(source.at[0, block], (here_k, here_v)[which][group].at[slot], left)
                )
                stores.append(pltpu.make_async_copy(source.at[1, block], there[group].at[which, slot], left))
    for store in stores:
        store.start()
    dq_ref[...] = dq_acc[...].astype(jnp.bfloat16)
    drk_ref[...] = drk_acc[...].astype(jnp.bfloat16)
    drv_ref[...] = drv_acc[...].astype(jnp.bfloat16)
    for store in stores:
        store.wait()


def attend(order, owners, spot, queries, cotangents, keys, values, gathered, head, joint, gates):
    rows = queries.shape[0]
    prompts, _, length, _ = gathered.shape
    deep = prompts // 8
    inward = pltpu.VMEM((4, prompts, length, HEAD), jnp.bfloat16)
    positions = 4 * length
    wide = PER_GROUP * HEAD
    here = lambda shape: pl.BlockSpec(shape, lambda i, *_: (0, head))
    out = lambda shape: pl.BlockSpec(shape, lambda i, *_: (0, 0))
    far = pl.BlockSpec(memory_space=pl.ANY)
    outward = pltpu.VMEM((2, 4, 4, deep, length, HEAD), jnp.bfloat16)
    share = jax.ShapeDtypeStruct((2, 4, deep, length, HEAD), jnp.bfloat16)
    return pl.pallas_call(
        functools.partial(attend_kernel, FIRST[head], head, joint),
        grid_spec=pltpu.PrefetchScalarGridSpec(
            num_scalar_prefetch=3,
            grid=(1,),
            in_specs=[here((rows, wide)), here((rows, wide)), here((rows, HEAD)), here((rows, HEAD))]
            + [far],
            out_specs=[out((rows, wide)), out((rows, HEAD)), out((rows, HEAD))] + [far] * (5 if joint else 6),
            scratch_shapes=[
                pltpu.VMEM((rows * PER_GROUP, HEAD), jnp.bfloat16),
                pltpu.VMEM((rows * PER_GROUP, HEAD), jnp.bfloat16),
                pltpu.VMEM((rows, HEAD), jnp.float32),
                pltpu.VMEM((rows, HEAD), jnp.float32),
                pltpu.VMEM((rows, wide), jnp.float32),
                pltpu.VMEM((rows, HEAD), jnp.float32),
                pltpu.VMEM((rows, HEAD), jnp.float32),
                inward,
                inward,
                outward,
                outward,
                pltpu.SemaphoreType.DMA,
                pltpu.SemaphoreType.DMA,
            ],
        ),
        out_shape=[
            jax.ShapeDtypeStruct((rows, wide), jnp.bfloat16),
            jax.ShapeDtypeStruct((rows, HEAD), jnp.bfloat16),
            jax.ShapeDtypeStruct((rows, HEAD), jnp.bfloat16),
        ]
        + [share] * 4
        + [jax.ShapeDtypeStruct((2, 2) + share.shape, jnp.bfloat16)] * joint
        + [jax.ShapeDtypeStruct((2,) + share.shape, jnp.bfloat16)] * (0 if joint else 2),
        compiler_params=pltpu.CompilerParams(vmem_limit_bytes=48 * 2**20),
        cost_estimate=pl.CostEstimate(
            flops=10 * rows * PER_GROUP * positions * HEAD,
            bytes_accessed=16 * prompts * positions * 2 * HEAD + 6 * rows * wide,
            transcendentals=rows * PER_GROUP * positions,
        ),
    )(after(order, *gates), owners, spot, queries, cotangents, keys, values, gathered)


def swap(array, axis, distance):
    count = lax.axis_size("wide") * lax.axis_size("narrow")
    flip = distance << BITS[axis]
    return lax.ppermute(array, ("wide", "narrow"), [(i, i ^ flip) for i in range(count)])


def other(axis):
    return "y" if axis == "x" else "x"


def after(value, *earlier):
    return lax.optimization_barrier((value, earlier))[0] if earlier else value


def sum_z(blocks):
    even, odd = blocks[0::2], blocks[1::2]
    pairs = even + swap(odd, "z", 1)
    total = pairs[0].astype(jnp.float32)
    for step in range(1, 4):
        total = total + swap(pairs[step], "z", 2 * step).astype(jnp.float32)
    return total.astype(jnp.bfloat16)


def halve_near(kept, sent, way, axis):
    got = swap(sent, axis, NEAR_FAR[way][0])
    return kept[0] + got[0], kept[1] + got[1]


def halve_far(mine, other_sum, way, axis):
    return mine + swap(other_sum, axis, NEAR_FAR[way][1])


def pick(blocks, which):
    return jnp.stack([blocks[b] for b in which])


WAYS = (0, 1)


def body(queries, output_gradient, response_keys, response_values, prompt_key_rows, prompt_value_rows, prompt_index):
    here = lax.axis_index("wide").astype(jnp.int32)
    order, owners = paired_order(prompt_index[:, 0])
    owners = owners ^ here
    spot = jnp.stack([lax.axis_index("narrow").astype(jnp.int32), here])

    held = jnp.concatenate([prompt_key_rows[0], prompt_value_rows[0]], axis=1)
    gathered = lax.all_gather(held, ("wide", "narrow"), axis=0, tiled=True)
    gathered = gathered.reshape(-1, 4, held.shape[0], held.shape[1])

    def run(head, *gates):
        return attend(
            order, owners, spot, queries, output_gradient, response_keys, response_values, gathered, head, head > 1, gates
        )

    results = {0: run(0)}
    results[1] = run(1, results[0][1])

    def over_core(heads, slot):
        there = {h: crossed[h][slot] if h in crossed else swap(results[h][7 + slot], "c", 1) for h in heads}
        return {(w, h): results[h][3 + 2 * w + slot] + there[h][w] for h in heads for w in WAYS}

    def near_first(sent):
        return {(w, h): swap(array, FIRST[h], NEAR_FAR[w][0]) for (w, h), array in sent.items()}

    def far_first(kept, got, *gates):
        out = {}
        for (w, h), mine in kept.items():
            far = after(mine[1] + got[w, h][1], *gates)
            out[w, h] = mine[0] + got[w, h][0] + swap(far, FIRST[h], NEAR_FAR[w][1])
        return out

    crossed = {}
    sent = over_core((0, 1), 1)
    got = near_first(sent)
    kept = over_core((0, 1), 0)
    results[2] = run(2, *sent.values(), kept[0, 0])
    results[3] = run(3, results[2][1])
    mine = far_first(kept, got, results[3][1])
    crossed = {h: swap(after(results[h][7], *got.values()), "c", 1) for h in (2, 3)}
    sent = over_core((2, 3), 1)
    got = near_first({key: after(array, *mine.values()) for key, array in sent.items()})
    kept = over_core((2, 3), 0)
    mine |= far_first(kept, got)
    total = {}
    for w in WAYS:
        for axis in ("x", "y"):
            heads = [h for h in range(KEY_VALUE_HEADS) if other(FIRST[h]) == axis]
            blocks = jnp.concatenate([mine[w, h] for h in heads], axis=-1)
            pairs = pick(blocks, KEEP_SEND[w][0]), pick(blocks, KEEP_SEND[w][1])
            result = halve_far(*halve_near(*pairs, w, axis), w, axis)
            for i, h in enumerate(heads):
                total[w, h] = result[..., i * HEAD : (i + 1) * HEAD]
    joined = jnp.concatenate([total[w, h] for w in WAYS for h in range(KEY_VALUE_HEADS)], axis=-1)
    summed = sum_z(joined)
    width = summed.shape[1] // 2
    key_sum, value_sum = summed[:, :width], summed[:, width:]
    dq, drk, drv = (jnp.concatenate([results[h][i] for h in range(KEY_VALUE_HEADS)], axis=1) for i in range(3))
    return dq, drk, drv, key_sum[None], value_sum[None]


def solution(mesh):
    spread = P(("wide", "narrow"), None)
    prompt = P("wide", "narrow", None)
    return jax.shard_map(
        body,
        mesh=mesh,
        in_specs=(spread, spread, spread, spread, prompt, prompt, spread),
        out_specs=(spread, spread, spread, prompt, prompt),
        check_vma=False,
    )
```

```python
import functools
import math

import jax
import jax.numpy as jnp
from jax import lax
from jax.experimental import pallas as pl
from jax.experimental.pallas import tpu as pltpu
from jax.sharding import PartitionSpec as P

QUERY_HEADS = 32
KEY_VALUE_HEADS = 4
PER_GROUP = QUERY_HEADS // KEY_VALUE_HEADS
HEAD = 128
TOKENS = 8
ROWS = PER_GROUP * TOKENS
SCALE = 1.0 / math.sqrt(HEAD)
LOG2E = math.log2(math.e)


def paired_order(targets):
    count = targets.shape[0]
    position = jnp.arange(count, dtype=jnp.int32)
    same = targets[:, None] == targets[None, :]
    before = position[None, :] < position[:, None]
    double = jnp.sum(same, axis=1) == 2
    first = jnp.logical_not(jnp.any(same & before, axis=1))
    head_of = jnp.sum(jnp.where(same & first[None, :], position[None, :], 0), axis=1)
    leads = double & first
    pair_rank = jnp.sum(leads[None, :] & (position[None, :] < head_of[:, None]), axis=1)
    single_rank = jnp.sum(jnp.logical_not(double)[None, :] & before, axis=1)
    slot = jnp.where(
        double,
        2 * pair_rank + jnp.logical_not(first).astype(jnp.int32),
        2 * jnp.sum(leads) + single_rank,
    )
    order = jnp.sum(jnp.where(slot[None, :] == position[:, None], position[None, :], 0), axis=1)
    owners = jnp.sum(jnp.where(slot[None, :] == position[:, None], targets[None, :], 0), axis=1)
    return order.astype(jnp.int32), owners.astype(jnp.int32)


def dot(left, right, contract):
    return lax.dot_general(left, right, (contract, ((), ())), preferred_element_type=jnp.float32)

KEEP_SEND = (((0, 3), (1, 2)), ((0, 1), (3, 2)))
NEAR_FAR = ((1, 3), (3, 1))
BITS = {"x": 0, "c": 2, "y": 3, "z": 5}
FIRST = ("x", "y", "x", "y")


def attend_kernel(first, head, joint, order, owners, spot, q_ref, d_ref, rk_ref, rv_ref, gathered, *refs):
    dq_ref, drk_ref, drv_ref = refs[:3]
    here_k, here_v, refs = refs[3:5], refs[5:7], refs[7:]
    there, refs = ((refs[0].at[0], refs[0].at[1]), refs[1:]) if joint else (refs[:2], refs[2:])
    q_rows, d_rows, own_k, own_v, dq_acc, drk_acc, drv_acc, k_in, v_in, dk_out, dv_out, arrived, left = refs
    responses = q_ref.shape[0] // TOKENS

    def place(g):
        core, y, z = g & 1, (g >> 1) & 3, g >> 3
        return (core, slice(None), y, z) if first == "x" else (core, y, slice(None), z)

    fetches = [
        pltpu.make_async_copy(
            gathered.at[:, spot[0] ^ block, :, pl.ds((KEY_VALUE_HEADS * which + head) * HEAD, HEAD)],
            (k_in, v_in)[which].at[block],
            arrived,
        )
        for which in range(2)
        for block in range(4)
    ]
    for fetch in fetches:
        fetch.start()

    def clear(g, _):
        for target in (dk_out, dv_out):
            for core in range(2):
                for block in range(4):
                    target[core, block, :, g] = jnp.zeros((4,) + target.shape[4:], target.dtype)
        return 0

    lax.fori_loop(0, dk_out.shape[3], clear, 0)
    own_k[...] = rk_ref[...].astype(jnp.float32)
    own_v[...] = rv_ref[...].astype(jnp.float32)

    def relay(p, _):
        lower = pl.multiple_of(p * 2 * TOKENS, 2 * TOKENS)
        for source, target in ((q_ref, q_rows), (d_ref, d_rows)):
            block = source[pl.ds(lower, 2 * TOKENS), :].astype(jnp.float32)
            stacked = jnp.concatenate(
                [
                    block[r * TOKENS : (r + 1) * TOKENS, h * HEAD : (h + 1) * HEAD]
                    for r in range(2)
                    for h in range(PER_GROUP)
                ],
                axis=0,
            )
            target[pl.ds(pl.multiple_of(p * 2 * ROWS, 2 * ROWS), 2 * ROWS), :] = stacked.astype(jnp.bfloat16)
        return 0

    lax.fori_loop(0, responses // 2, relay, 0)
    for fetch in fetches:
        fetch.wait()

    lanes = 2 * ROWS
    key_at = lax.broadcasted_iota(jnp.int32, (TOKENS, lanes), 0)
    token_at = lax.rem(lax.broadcasted_iota(jnp.int32, (TOKENS, lanes), 1), TOKENS)
    visible = key_at <= token_at
    none = jnp.zeros((ROWS, HEAD), jnp.bfloat16)
    blank = jnp.zeros((TOKENS, 2 * HEAD), jnp.float32)
    blank_lanes = jnp.zeros((TOKENS, lanes), jnp.float32)

    def both(a, b, axis):
        return jnp.concatenate([a, b], axis=axis)

    def visit(i, _):
        a, b = order[2 * i], order[2 * i + 1]
        ga, gb = owners[2 * i], owners[2 * i + 1]

        def take(scratch, g):
            return scratch[:, g ^ spot[1]].reshape(-1, HEAD)

        def give(scratch, g, rows):
            scratch[place(g)] = rows.astype(jnp.bfloat16).reshape((4,) + scratch.shape[4:])

        def spread(rows):
            first = rows[pl.ds(pl.multiple_of(a * ROWS, ROWS), ROWS), :]
            second = rows[pl.ds(pl.multiple_of(b * ROWS, ROWS), ROWS), :]
            return both(both(first, none, 1), both(none, second, 1), 0)

        at_a = pl.ds(pl.multiple_of(a * TOKENS, TOKENS), TOKENS)
        at_b = pl.ds(pl.multiple_of(b * TOKENS, TOKENS), TOKENS)
        q, d = spread(q_rows), spread(d_rows)
        k = both(take(k_in, ga), take(k_in, gb), 1)
        v = both(take(v_in, ga), take(v_in, gb), 1)
        ko = both(both(own_k[at_a, :], own_k[at_b, :], 1), blank, 0).astype(jnp.bfloat16)
        vo = both(both(own_v[at_a, :], own_v[at_b, :], 1), blank, 0).astype(jnp.bfloat16)
        across, along = ((1,), (1,)), ((1,), (0,))
        s = dot(k, q, across)
        t = dot(v, d, across)
        so = jnp.where(visible, dot(ko, q, across)[:TOKENS], -1e30)
        to = dot(vo, d, across)[:TOKENS]
        top = jnp.maximum(jnp.max(s, axis=0, keepdims=True), jnp.max(so, axis=0, keepdims=True))
        e = jnp.exp2((s - top) * (SCALE * LOG2E))
        eo = jnp.exp2((so - top) * (SCALE * LOG2E))
        total = jnp.sum(e, axis=0, keepdims=True) + jnp.sum(eo, axis=0, keepdims=True)
        mixed = jnp.sum(e * t, axis=0, keepdims=True) + jnp.sum(eo * to, axis=0, keepdims=True)
        inverse = 1.0 / total
        delta = mixed * inverse
        p = e * inverse
        po = eo * inverse
        w = p.astype(jnp.bfloat16)
        ds = (p * (t - delta)).astype(jnp.bfloat16)
        wo = both(po, blank_lanes, 0).astype(jnp.bfloat16)
        dso = both(po * (to - delta), blank_lanes, 0).astype(jnp.bfloat16)
        dk = dot(ds, q, along) * SCALE
        dv = dot(w, d, along)
        dko = dot(dso, q, along)[:TOKENS] * SCALE
        dvo = dot(wo, d, along)[:TOKENS]
        down = ((0,), (0,))
        dq = (dot(ds, k, down) + dot(dso, ko, down)) * SCALE
        for at, rows in ((at_a, dq[:ROWS, :HEAD]), (at_b, dq[ROWS:, HEAD:])):
            dq_acc[at, :] = jnp.concatenate(
                [rows[h * TOKENS : (h + 1) * TOKENS] for h in range(PER_GROUP)], axis=1
            )
        drk_acc[at_a, :] = dko[:, :HEAD]
        drk_acc[at_b, :] = dko[:, HEAD:]
        drv_acc[at_a, :] = dvo[:, :HEAD]
        drv_acc[at_b, :] = dvo[:, HEAD:]
        shared = (ga == gb).astype(jnp.float32)
        give(dk_out, gb, dk[:, HEAD:])
        give(dv_out, gb, dv[:, HEAD:])
        give(dk_out, ga, dk[:, :HEAD] + shared * dk[:, HEAD:])
        give(dv_out, ga, dv[:, :HEAD] + shared * dv[:, HEAD:])
        return 0

    lax.fori_loop(0, responses // 2, visit, 0, unroll=3)
    stores = []
    for which in range(2):
        for group in range(2):
            for slot, block in enumerate(KEEP_SEND[which][group]):
                source = (dk_out, dv_out)[which]
                stores.append(
                    pltpu.make_async_copy(source.at[0, block], (here_k, here_v)[which][group].at[slot], left)
                )
                stores.append(pltpu.make_async_copy(source.at[1, block], there[group].at[which, slot], left))
    for store in stores:
        store.start()
    dq_ref[...] = dq_acc[...].astype(jnp.bfloat16)
    drk_ref[...] = drk_acc[...].astype(jnp.bfloat16)
    drv_ref[...] = drv_acc[...].astype(jnp.bfloat16)
    for store in stores:
        store.wait()


def attend(order, owners, spot, queries, cotangents, keys, values, gathered, head, joint, gates):
    rows = queries.shape[0]
    prompts, _, length, _ = gathered.shape
    deep = prompts // 8
    inward = pltpu.VMEM((4, prompts, length, HEAD), jnp.bfloat16)
    positions = 4 * length
    wide = PER_GROUP * HEAD
    here = lambda shape: pl.BlockSpec(shape, lambda i, *_: (0, head))
    out = lambda shape: pl.BlockSpec(shape, lambda i, *_: (0, 0))
    far = pl.BlockSpec(memory_space=pl.ANY)
    outward = pltpu.VMEM((2, 4, 4, deep, length, HEAD), jnp.bfloat16)
    share = jax.ShapeDtypeStruct((2, 4, deep, length, HEAD), jnp.bfloat16)
    return pl.pallas_call(
        functools.partial(attend_kernel, FIRST[head], head, joint),
        grid_spec=pltpu.PrefetchScalarGridSpec(
            num_scalar_prefetch=3,
            grid=(1,),
            in_specs=[here((rows, wide)), here((rows, wide)), here((rows, HEAD)), here((rows, HEAD))]
            + [far],
            out_specs=[out((rows, wide)), out((rows, HEAD)), out((rows, HEAD))] + [far] * (5 if joint else 6),
            scratch_shapes=[
                pltpu.VMEM((rows * PER_GROUP, HEAD), jnp.bfloat16),
                pltpu.VMEM((rows * PER_GROUP, HEAD), jnp.bfloat16),
                pltpu.VMEM((rows, HEAD), jnp.float32),
                pltpu.VMEM((rows, HEAD), jnp.float32),
                pltpu.VMEM((rows, wide), jnp.float32),
                pltpu.VMEM((rows, HEAD), jnp.float32),
                pltpu.VMEM((rows, HEAD), jnp.float32),
                inward,
                inward,
                outward,
                outward,
                pltpu.SemaphoreType.DMA,
                pltpu.SemaphoreType.DMA,
            ],
        ),
        out_shape=[
            jax.ShapeDtypeStruct((rows, wide), jnp.bfloat16),
            jax.ShapeDtypeStruct((rows, HEAD), jnp.bfloat16),
            jax.ShapeDtypeStruct((rows, HEAD), jnp.bfloat16),
        ]
        + [share] * 4
        + [jax.ShapeDtypeStruct((2, 2) + share.shape, jnp.bfloat16)] * joint
        + [jax.ShapeDtypeStruct((2,) + share.shape, jnp.bfloat16)] * (0 if joint else 2),
        compiler_params=pltpu.CompilerParams(vmem_limit_bytes=48 * 2**20),
        cost_estimate=pl.CostEstimate(
            flops=10 * rows * PER_GROUP * positions * HEAD,
            bytes_accessed=16 * prompts * positions * 2 * HEAD + 6 * rows * wide,
            transcendentals=rows * PER_GROUP * positions,
        ),
    )(after(order, *gates), owners, spot, queries, cotangents, keys, values, gathered)


def swap(array, axis, distance):
    count = lax.axis_size("wide") * lax.axis_size("narrow")
    flip = distance << BITS[axis]
    return lax.ppermute(array, ("wide", "narrow"), [(i, i ^ flip) for i in range(count)])


def other(axis):
    return "y" if axis == "x" else "x"


def after(value, *earlier):
    return lax.optimization_barrier((value, earlier))[0] if earlier else value


def sum_z(blocks):
    even, odd = blocks[0::2], blocks[1::2]
    pairs = even + swap(odd, "z", 1)
    total = pairs[0].astype(jnp.float32)
    for step in range(1, 4):
        total = total + swap(pairs[step], "z", 2 * step).astype(jnp.float32)
    return total.astype(jnp.bfloat16)


def halve_near(kept, sent, way, axis):
    got = swap(sent, axis, NEAR_FAR[way][0])
    return kept[0] + got[0], kept[1] + got[1]


def halve_far(mine, other_sum, way, axis):
    return mine + swap(other_sum, axis, NEAR_FAR[way][1])


def pick(blocks, which):
    return jnp.stack([blocks[b] for b in which])


WAYS = (0, 1)


def body(queries, output_gradient, response_keys, response_values, prompt_key_rows, prompt_value_rows, prompt_index):
    here = lax.axis_index("wide").astype(jnp.int32)
    order, owners = paired_order(prompt_index[:, 0])
    owners = owners ^ here
    spot = jnp.stack([lax.axis_index("narrow").astype(jnp.int32), here])

    held = jnp.concatenate([prompt_key_rows[0], prompt_value_rows[0]], axis=1)
    gathered = lax.all_gather(held, ("wide", "narrow"), axis=0, tiled=True)
    gathered = gathered.reshape(-1, 4, held.shape[0], held.shape[1])

    def run(head, *gates):
        return attend(
            order, owners, spot, queries, output_gradient, response_keys, response_values, gathered, head, head > 1, gates
        )

    results = {0: run(0)}
    results[1] = run(1, results[0][1])

    def over_core(heads, slot):
        there = {h: crossed[h][slot] if h in crossed else swap(results[h][7 + slot], "c", 1) for h in heads}
        return {(w, h): results[h][3 + 2 * w + slot] + there[h][w] for h in heads for w in WAYS}

    def near_first(sent):
        return {(w, h): swap(array, FIRST[h], NEAR_FAR[w][0]) for (w, h), array in sent.items()}

    def far_first(kept, got, *gates):
        out = {}
        for (w, h), mine in kept.items():
            far = after(mine[1] + got[w, h][1], *gates)
            out[w, h] = mine[0] + got[w, h][0] + swap(far, FIRST[h], NEAR_FAR[w][1])
        return out

    crossed = {}
    sent = over_core((0, 1), 1)
    got = near_first(sent)
    kept = over_core((0, 1), 0)
    results[2] = run(2, *sent.values(), kept[0, 0])
    results[3] = run(3, results[2][1])
    mine = far_first(kept, got, results[3][1])
    crossed = {2: swap(after(results[2][7], *got.values(), results[3][1]), "c", 1)}
    crossed[3] = swap(after(results[3][7], crossed[2]), "c", 1)
    sent = over_core((2, 3), 1)
    got = near_first({key: after(array, *mine.values(), *sent.values()) for key, array in sent.items()})
    kept = over_core((2, 3), 0)
    mine |= far_first(kept, got)
    total = {}
    for w in WAYS:
        for axis in ("x", "y"):
            heads = [h for h in range(KEY_VALUE_HEADS) if other(FIRST[h]) == axis]
            blocks = jnp.concatenate([mine[w, h] for h in heads], axis=-1)
            pairs = pick(blocks, KEEP_SEND[w][0]), pick(blocks, KEEP_SEND[w][1])
            result = halve_far(*halve_near(*pairs, w, axis), w, axis)
            for i, h in enumerate(heads):
                total[w, h] = result[..., i * HEAD : (i + 1) * HEAD]
    joined = jnp.concatenate([total[w, h] for w in WAYS for h in range(KEY_VALUE_HEADS)], axis=-1)
    summed = sum_z(joined)
    width = summed.shape[1] // 2
    key_sum, value_sum = summed[:, :width], summed[:, width:]
    dq, drk, drv = (jnp.concatenate([results[h][i] for h in range(KEY_VALUE_HEADS)], axis=1) for i in range(3))
    return dq, drk, drv, key_sum[None], value_sum[None]


def solution(mesh):
    spread = P(("wide", "narrow"), None)
    prompt = P("wide", "narrow", None)
    return jax.shard_map(
        body,
        mesh=mesh,
        in_specs=(spread, spread, spread, spread, prompt, prompt, spread),
        out_specs=(spread, spread, spread, prompt, prompt),
        check_vma=False,
    )
```
